256 devices in a mesh: rep: 8 (over y, core), fsdp: 32 (over z, x).
Axes of the slice: x: 4, y: 4, z: 8, core: 2. Of those that a mesh axis runs over, the one named last changes fastest.
Arguments:
- tokens: bfloat16 [147456, 512], P(('rep', 'fsdp')), may hold values from -6 to 6
- cotangent: bfloat16 [147456, 512], P(('rep', 'fsdp')), may hold values from -6 to 6
- window_order: int32 [256, 576], P(('rep', 'fsdp')), may hold values from 0 to 575, each once within a row
- gain: float32 [512], replicated, may hold values from 0.1 to 1.9
- w_qkv: bfloat16 [512, 1536], P('fsdp'), may hold values from -8 to 8
- w_out: bfloat16 [512, 512], P('fsdp'), may hold values from -0.25 to 0.25
- err_qkv: float32 [8, 512, 1536], P('rep', 'fsdp'), may hold values from -6 to 6
- err_out: float32 [8, 512, 512], P('rep', 'fsdp'), may hold values from -6 to 6
- q_qkv: int32 [1536, 32], replicated, may hold values from -127 to 127
- q_out: int32 [512, 32], replicated, may hold values from -127 to 127
Outputs:
- d_tokens: bfloat16 [147456, 512], P(('rep', 'fsdp'))
- grad_qkv: float32 [512, 1536], P('fsdp')
- grad_out: float32 [512, 512], P('fsdp')
- err_qkv_next: float32 [8, 512, 1536], P('rep', 'fsdp')
- err_out_next: float32 [8, 512, 512], P('rep', 'fsdp')
- basis_qkv_next: float32 [1536, 32], replicated
- basis_out_next: float32 [512, 32], replicated
The draws below stay inside these ranges and needn't reach their ends.
Inputs may be any that keep to these rules, and one draw needn't show every extreme that they name: `window_order`: each row is a permutation of 0 to 575.
All inputs are finite; a program needn't handle non-finite values.
Results may differ from the reference program's by a relative error of at most 0.017.
Values may be sent and summed in bfloat16 or wider, within the bound.
A program may use at most 64 MiB of HBM per device.

```python
import jax
import jax.numpy as jnp
from jax import lax

D = 512
HEADS = 8
WT = 144
RANK = 32
TOK_DEV = 576
TOKENS = 147456
N_REP = 8
N_FSDP = 32
DEVICES = 256


def draw_w_qkv(key, part):
    key = jax.random.fold_in(key, 7)
    base = jnp.clip(jax.random.normal(key, (D, 3 * D), jnp.float32), -5.0, 5.0) * D ** (-0.5)
    return base.astype(jnp.bfloat16)


def with_ends(drawn, rng, smallest, top_value):
    longest = drawn.shape.index(max(drawn.shape))
    spots = []
    for shift in (0, 1):
        where = [jax.random.randint(jax.random.fold_in(rng, axis), (), 0, length) for axis, length in enumerate(drawn.shape)]
        where[longest] = (where[longest] + shift) % drawn.shape[longest]
        spots.append(tuple(where))
    return drawn.at[spots[0]].set(smallest).at[spots[1]].set(top_value)


def levels(rng, shape, split, smallest, largest):
    factor_of, own = 1.0, jax.random.fold_in(rng, 6)
    for position, shards_of in split:
        draws = jnp.exp(jax.random.uniform(jax.random.fold_in(own, position), (shards_of,), jnp.float32, smallest / len(split), largest / len(split)))
        factor_of = factor_of * jnp.repeat(draws, shape[position] // shards_of).reshape([-1 if axis == position else 1 for axis in range(len(shape))])
    return factor_of


def gaussian(key, extent, scale, limit, split=(), kind=jnp.bfloat16):
    loudness = levels(key, extent, split, -0.22, 0.18) if split else 1.0
    array = jax.random.normal(key, extent, jnp.float32) * scale * loudness
    return jnp.minimum(jnp.maximum(array, -limit), limit).astype(kind)


def setup_inputs(seed: int = 0) -> dict:
    streams_of = jax.random.split(jax.random.key(seed), 11)
    return {
        "tokens": gaussian(streams_of[0], (TOKENS, D), 1.0, 6.0, ((0, 256),)),
        "cotangent": gaussian(streams_of[1], (TOKENS, D), 1.0, 6.0, ((0, 256),)),
        "window_order": jax.vmap(lambda own: jax.random.permutation(own, TOK_DEV))(jax.random.split(streams_of[2], DEVICES)).reshape((DEVICES, TOK_DEV)).astype(jnp.int32),
        "gain": jnp.clip(1.0 + 0.18 * jax.random.normal(streams_of[3], (D,), jnp.float32), 0.1, 1.9),
        "w_qkv": draw_w_qkv(jax.random.fold_in(streams_of[10], 71), 0),
        "w_out": gaussian(streams_of[5], (D, D), D ** -0.5, 0.25, ((0, 32),)),
        "err_qkv": gaussian(streams_of[6], (N_REP, D, 3 * D), 1.0, 6.0, ((0, 8), (1, 32)), jnp.float32),
        "err_out": gaussian(streams_of[7], (N_REP, D, D), 1.0, 6.0, ((0, 8), (1, 32)), jnp.float32),
        "q_qkv": with_ends(jax.random.randint(streams_of[8], (3 * D, RANK), -127, 128), jax.random.fold_in(streams_of[8], 1), -127, 127).astype(jnp.int32),
        "q_out": with_ends(jax.random.randint(streams_of[9], (D, RANK), -127, 128), jax.random.fold_in(streams_of[9], 1), -127, 127).astype(jnp.int32),
    }


def layer_norm(values, gain):
    center = values - lax.optimization_barrier(jnp.mean(values, -1, keepdims=True))
    spread = lax.optimization_barrier(jnp.mean(center * center, -1, keepdims=True))
    return (center * lax.rsqrt(spread + 1e-05) * gain).astype(jnp.bfloat16)

def attend(qkv, heads):
    count, span, triple = qkv.shape
    width = triple // 3
    size = width // heads
    parts = qkv.reshape(count, span, 3, heads, size).astype(jnp.float32)
    query = parts[:, :, 0]
    key_part = parts[:, :, 1]
    value = parts[:, :, 2]
    scores = jnp.einsum('nqhd,nkhd->nhqk', query, key_part) * size ** (-0.5)
    top = lax.optimization_barrier(jnp.max(scores, -1, keepdims=True))
    weights = jnp.exp(scores - top)
    weights = weights / lax.optimization_barrier(jnp.sum(weights, -1, keepdims=True))
    probs = lax.optimization_barrier(weights.astype(jnp.bfloat16)).astype(jnp.float32)
    context = jnp.einsum('nhqk,nkhd->nqhd', probs, value)
    return context.astype(jnp.bfloat16).reshape(count, span, width)

def compress(grads, errors, integers):
    highest = lax.Precision.HIGHEST
    total = grads + errors
    basis = integers.astype(jnp.float32) / 127.0
    left = lax.optimization_barrier(jnp.mean(jnp.einsum('rij,jk->rik', total, basis, precision=highest), axis=0))
    gram = jnp.dot(left.T, left, precision=highest)
    lower = jnp.linalg.cholesky(gram)
    ortho = jax.scipy.linalg.solve_triangular(lower, left.T, lower=True).T
    right = lax.optimization_barrier(jnp.mean(jnp.einsum('rij,ik->rjk', total, ortho, precision=highest), axis=0))
    approx = jnp.dot(ortho, right.T, precision=highest)
    return (approx, total - approx[None], right)

def reference(tokens, cotangent, window_order, gain, w_qkv, w_out, err_qkv, err_out, q_qkv, q_out):
    scale = float(N_FSDP * TOK_DEV) ** (-0.5)
    offsets = (jnp.arange(N_REP * N_FSDP, dtype=jnp.int32) * TOK_DEV)[:, None]
    index = (window_order.astype(jnp.int32) + offsets).reshape(N_REP, N_FSDP * TOK_DEV)

    def replica(positions):
        rows = jnp.take(tokens, positions, axis=0)
        back = jnp.take(cotangent, positions, axis=0)
        normed, norm_back = jax.vjp(lambda v: layer_norm(v, gain), rows.astype(jnp.float32))
        qkv = jnp.dot(normed.astype(jnp.float32), w_qkv.astype(jnp.float32), preferred_element_type=jnp.float32).astype(jnp.bfloat16)
        context, attend_back = jax.vjp(lambda a: attend(a.reshape(-1, WT, 3 * D), HEADS).reshape(-1, D), qkv)
        g_out = jnp.dot(context.T.astype(jnp.float32), back.astype(jnp.float32), preferred_element_type=jnp.float32) * scale
        d_context = jnp.dot(back.astype(jnp.float32), w_out.T.astype(jnp.float32), preferred_element_type=jnp.float32).astype(jnp.bfloat16)
        d_qkv = attend_back(d_context)[0]
        g_qkv = jnp.dot(normed.T.astype(jnp.float32), d_qkv.astype(jnp.float32), preferred_element_type=jnp.float32) * scale
        d_normed = jnp.dot(d_qkv.astype(jnp.float32), w_qkv.T.astype(jnp.float32), preferred_element_type=jnp.float32).astype(jnp.bfloat16)
        d_rows = norm_back(d_normed)[0]
        d_win = (back.astype(jnp.float32) + d_rows).astype(jnp.bfloat16)
        return (g_qkv, g_out, d_win)
    g_qkv, g_out, d_win = lax.map(replica, index)
    d_tokens = jnp.zeros_like(tokens).at[index.reshape(-1)].set(d_win.reshape(-1, D))
    grad_qkv, err_qkv_next, basis_qkv_next = compress(g_qkv, err_qkv, q_qkv)
    grad_out, err_out_next, basis_out_next = compress(g_out, err_out, q_out)
    return (d_tokens, grad_qkv, grad_out, err_qkv_next, err_out_next, basis_qkv_next, basis_out_next)
```

```python
import functools

import jax
import jax.numpy as jnp
from jax import lax
from jax.experimental import pallas as pl
from jax.experimental.pallas import tpu as pltpu
from jax.sharding import PartitionSpec as P

f32 = jnp.float32
bf16 = jnp.bfloat16
MESH = pl.DeviceIdType.MESH
HI = lax.Precision.HIGHEST
def dot(a,b): return jnp.dot(a,b,preferred_element_type=f32)
def dnt(a,b): return lax.dot_general(a,b,(((1,),(1,)),((),())),preferred_element_type=f32)
WT=144; NW=4
LOG2E=1.4426950408889634
def front_window(w,order_ref,tok_ref,cot_ref,gain_ref,back_ref,n_ref,xh_ref,rstd_ref):
        row=order_ref[...]
        T=row.shape[1]
        gain=gain_ref[...]
        sl=pl.ds(w*WT,WT)
        si=lax.broadcasted_iota(jnp.int32,(WT,T),0)+w*WT
        li=lax.broadcasted_iota(jnp.int32,(WT,T),1)
        col=jnp.sum(jnp.where(si==li,row,0).astype(f32),axis=1,keepdims=True).astype(jnp.int32)
        oh=jnp.where(col==li,1.0,0.0).astype(bf16)
        x=dot(oh,tok_ref[...])
        back_ref[sl,:]=dot(oh,cot_ref[...]).astype(bf16)
        ce=x-jnp.mean(x,-1,keepdims=True)
        rs=lax.rsqrt(jnp.mean(ce*ce,-1,keepdims=True)+1e-5)
        xh=ce*rs
        xh_ref[sl,:]=xh
        rstd_ref[sl,:]=rs
        n=(xh*gain).astype(bf16)
        n_ref[sl,:]=n
def pair(n_ref,nt_ref,back_ref,W,WO,d_ref,dn_ref,qkvc_ref,scale,first,g_store,go_store,mid=None):
    qkvc_ref[:,:384]=dot(n_ref[...],W).astype(bf16)
    qkvc_ref[:,384:]=dnt(back_ref[...],WO).astype(bf16)
    if mid is not None: mid()
    lane=lax.broadcasted_iota(jnp.int32,(WT,128),1)
    go=jnp.zeros((128,512),f32)
    for w in range(NW):
        sl=pl.ds(w*WT,WT)
        q=qkvc_ref[sl,0:128]; k=qkvc_ref[sl,128:256]; v=qkvc_ref[sl,256:384]; c=qkvc_ref[sl,384:512]
        qt=q.T; kt=k.T; vt=v.T; ct=c.T
        cts=[];dqs=[]
        dv=jnp.zeros((WT,128),f32); dk=jnp.zeros((WT,128),f32)
        for h in range(2):
            m=(lane<64) if h==0 else (lane>=64)
            z=jnp.zeros((),bf16)
            s=dot(jnp.where(m,k,z),qt)
            mx=jnp.max(s,axis=0,keepdims=True)
            e=jnp.exp2((s-mx)*(0.125*LOG2E))
            wt=e*(1.0/jnp.sum(e,axis=0,keepdims=True))
            p=wt.astype(bf16)
            cts.append(dot(vt[64*h:64*h+64],p))
            dp=dot(jnp.where(m,v,z),ct).astype(bf16).astype(f32)
            t=wt*dp
            ds=(t-wt*jnp.sum(t,axis=0,keepdims=True)).astype(bf16)
            dv=dv+dot(p,jnp.where(m,c,z))
            dk=dk+dot(ds,jnp.where(m,q,z))
            dqs.append(dot(kt[64*h:64*h+64],ds))
        ctx=jnp.concatenate(cts,0).astype(bf16)
        go=go+dot(ctx,back_ref[sl,:])
        dq=(jnp.concatenate(dqs,0)*0.125).astype(bf16).T
        d_ref[sl,0:128]=dq
        d_ref[sl,128:256]=(dk*0.125).astype(bf16)
        d_ref[sl,256:384]=dv.astype(bf16)
    go_store((go*scale).astype(bf16))
    g_store((dot(nt_ref[...],d_ref[...])*scale).astype(bf16))
    dn=dnt(d_ref[...],W)
    dn_ref[...]=jnp.where(first,0.0,dn_ref[...])+dn
def tail_norm(dn_ref,xh_ref,rstd_ref,gain_ref,back_ref,dwin_ref):
    gain=gain_ref[...]
    for w in range(NW):
        sl=pl.ds(w*WT,WT)
        dx=dn_ref[sl,:].astype(bf16).astype(f32)*gain
        xh=xh_ref[sl,:]
        d=rstd_ref[sl,:]*(dx-jnp.mean(dx,-1,keepdims=True)-xh*jnp.mean(dx*xh,-1,keepdims=True))
        dwin_ref[sl,:]=(back_ref[sl,:].astype(f32)+d).astype(bf16)

def tail_put(order_ref,dwin_ref,out_ref):
    row=order_ref[...]
    T=row.shape[1]
    for w in range(NW):
        sl=pl.ds(w*WT,WT)
        si=lax.broadcasted_iota(jnp.int32,(WT,T),0)+w*WT
        oh=jnp.where(si==row,1.0,0.0).astype(bf16)
        out_ref[sl,:]=dot(oh,dwin_ref[...]).astype(bf16)


def dnt_hi(a, b):
    return lax.dot_general(a, b, (((1,), (1,)), ((), ())), precision=HI, preferred_element_type=f32)


def remote(src, dst, ss, rs, dev):
    return pltpu.make_async_remote_copy(
        src_ref=src, dst_ref=dst, send_sem=ss, recv_sem=rs, device_id=dev, device_id_type=MESH
    )


def hdot(a, b):
    return jnp.dot(a, b, precision=HI, preferred_element_type=f32)


def split3(v):
    a = v.astype(bf16)
    r = v - a.astype(f32)
    b = r.astype(bf16)
    c = (r - b.astype(f32)).astype(bf16)
    return jnp.concatenate([a, b, c], 0)


def inverse_factors(gram):
    lane = lax.broadcasted_iota(jnp.int32, (32, 128), 1)
    row = lax.broadcasted_iota(jnp.int32, (32, 128), 0)
    first = (lane % 64) < 32
    state = jnp.where(lane < 64, gram, jnp.where((lane % 32) == row, 1.0, 0.0))
    for j in range(31):
        cols = jnp.where(first, state[:, j : j + 1], state[:, 32 + j : 33 + j])
        factor = cols / cols[j : j + 1, :]
        state = state - jnp.where(row > j, factor, 0.0) * state[j : j + 1, :]
    out = []
    for k in range(2):
        diag = jnp.sum(jnp.where(lane == row + 32 * k, state, 0.0), axis=1, keepdims=True)
        out.append(state[:, 64 + 32 * k : 96 + 32 * k] * (1.0 / jnp.sqrt(diag)))
    return out


def kernel(
    scale,
    order_ref, tok_ref, cot_ref, gain_ref, w_ref, wo_ref, errq_ref, erro_ref, qq_ref, qo_ref,
    dtok_ref, gradq_ref, grado_ref, nerrq_ref, nerro_ref, bq_ref, bo_ref,
    W, WO, back, n, nt, xh, rstd, d, dn, qkvc,
    gbuf, xr, zs, zr, gobuf, xro, zso, zro, mq, mo,
    lr, gx, gz, tb, er1, t1, ex, t2, ey, ez, R,
    az_s, az_r, ax_s, ax_r, ay_s, ay_r, ac_s, ac_r,
    rx_s, rx_r, rz_s, rz_r, ro_s,
    l_s, l_r, gx_s, gx_r, gz_s, gz_r, e_s, e_r,
):
    r = lax.axis_index("rep")
    f = lax.axis_index("fsdp")
    y = r // 2
    c = r % 2
    z = f // 4
    x = f % 4

    def zp(dz):
        return (r, ((z + dz) % 8) * 4 + x)

    def xp(dx):
        return (r, z * 4 + (x + dx) % 4)

    def yp(dy):
        return (((y + dy) % 4) * 2 + c, f)

    cp = (y * 2 + 1 - c, f)

    def rp(k):
        return ((r + k) % 8, f)

    barrier = pltpu.get_barrier_semaphore()
    for k in range(1, 8):
        pl.semaphore_signal(barrier, inc=1, device_id=zp(k), device_id_type=MESH)
        pl.semaphore_signal(barrier, inc=1, device_id=rp(k), device_id_type=MESH)
    for k in range(1, 4):
        pl.semaphore_signal(barrier, inc=1, device_id=xp(k), device_id_type=MESH)

    def fr(w):
        front_window(w, order_ref, tok_ref, cot_ref, gain_ref, back, n, xh, rstd)

    source = (x // 2) == c

    @pl.when(source)
    def _():
        for k in range(3):
            W[y, z, x, :, 128 * k : 128 * k + 128] = w_ref[
                :, pl.ds(pl.multiple_of(512 * k + y * 128, 128), 128)
            ]

        @pl.when((z // 2) == y)
        def _():
            WO[z, x] = wo_ref[...]

    fr(0)
    pl.semaphore_wait(barrier, 17)

    @pl.when(source)
    def _():
        for k in range(1, 8):
            remote(W.at[y, z, x], W.at[y, z, x], az_s.at[0, k - 1], az_r.at[0, k - 1], zp(k)).start()

        @pl.when((z // 2) == y)
        def _():
            for k in range(1, 8):
                remote(WO.at[z, x], WO.at[z, x], az_s.at[1, k - 1], az_r.at[1, k - 1], zp(k)).start()

    fr(1)
    fr(2)

    @pl.when(source)
    def _():
        for k in range(1, 8):
            src = (z - k + 8) % 8
            remote(W.at[y, src, x], W.at[y, src, x], az_s.at[0, k - 1], az_r.at[0, k - 1], zp(k)).wait_recv()

            @pl.when((src // 2) == y)
            def _():
                remote(WO.at[src, x], WO.at[src, x], az_s.at[1, k - 1], az_r.at[1, k - 1], zp(k)).wait_recv()

        for k in range(1, 4):
            remote(W.at[y, :, x], W.at[y, :, x], ax_s.at[0, k - 1], ax_r.at[0, k - 1], xp(k)).start()
            o = WO.at[pl.ds(2 * y, 2), x]
            remote(o, o, ax_s.at[1, k - 1], ax_r.at[1, k - 1], xp(k)).start()

    fr(3)
    nt[...] = n[...].T

    for k in range(1, 4):
        src = (x - k + 4) % 4

        @pl.when((src // 2) == c)
        def _():
            remote(W.at[y, :, src], W.at[y, :, src], ax_s.at[0, k - 1], ax_r.at[0, k - 1], xp(k)).wait_recv()
            o = WO.at[pl.ds(2 * y, 2), src]
            remote(o, o, ax_s.at[1, k - 1], ax_r.at[1, k - 1], xp(k)).wait_recv()

    def dy_of(s):
        return s + (s // 2) * (1 - 2 * (s % 2))

    def hp_of(s):
        return (y - dy_of(s) + 4) % 4

    def half(hp, core):
        return W.at[hp, :, pl.ds(2 * core, 2)], WO.at[pl.ds(2 * hp, 2), pl.ds(2 * core, 2)]

    def core_copy(s, core):
        a, b = half(hp_of(s), core)
        return (
            remote(a, a, ac_s.at[0, s], ac_r.at[0, s], cp),
            remote(b, b, ac_s.at[1, s], ac_r.at[1, s], cp),
        )

    def y_copy(dy, hp):
        a, b = half(hp, c)
        return (
            remote(a, a, ay_s.at[0, dy - 1], ay_r.at[0, dy - 1], yp(dy)),
            remote(b, b, ay_s.at[1, dy - 1], ay_r.at[1, dy - 1], yp(dy)),
        )

    for cc in core_copy(0, c):
        cc.start()
    for dy in (1, 3, 2):
        for cc in y_copy(dy, y):
            cc.start()

    def x_send(s, k):
        to = (x + k) % 4
        return (
            remote(gbuf.at[s, :, to], xr.at[s, k - 1], rx_s.at[0, s, k - 1], rx_r.at[0, s, k - 1], xp(k)),
            remote(gobuf.at[s, :, to], xro.at[s, k - 1], rx_s.at[1, s, k - 1], rx_r.at[1, s, k - 1], xp(k)),
        )

    def z_send(s, k):
        return remote(
            zs.at[s, (z + k) % 8], zr.at[s, k - 1], rz_s.at[0, s, k - 1], rz_r.at[0, s, k - 1], zp(k)
        )

    def zo_send(s, j, k):
        return remote(zso.at[s, j], zro.at[k - 1], ro_s.at[s, j], rz_r.at[1, 0, k - 1], zp(k))

    def zo_each(s, act):
        for j in range(2):
            k = (2 * hp_of(s) + j - z + 8) % 8

            @pl.when(k > 0)
            def _():
                act(zo_send(s, j, k))

    def second(s):
        for k in range(1, 4):
            for cc in x_send(s, k):
                cc.wait_recv()
        total = gbuf[s, :, x].astype(f32)
        totalo = gobuf[s, :, x].astype(f32)
        for k in range(3):
            total = total + xr[s, k].astype(f32)
            totalo = totalo + xro[s, k].astype(f32)
        zs[s] = total.astype(bf16)
        zso[s] = totalo.astype(bf16)
        for k in range(1, 8):
            z_send(s, k).start()
        zo_each(s, lambda cc: cc.start())

    def step(s, carry):
        hp = hp_of(s)
        for cc in core_copy(s, 1 - c):
            cc.wait_recv()

        def mid():
            @pl.when(s < 3)
            def _():
                dy = dy_of(s + 1)
                for cc in y_copy(dy, hp_of(s + 1)):
                    cc.wait_recv()
                for cc in core_copy(s + 1, c):
                    cc.start()

        def g_store(v):
            gbuf[s] = v.reshape(8, 4, 16, 384)

        def go_store(v):
            gobuf[s] = v.reshape(2, 4, 16, 512)

        pair(
            n, nt, back, W[hp].reshape(512, 384), WO[pl.ds(2 * hp, 2)].reshape(128, 512),
            d, dn, qkvc, scale, s == 0, g_store, go_store, mid,
        )
        for k in range(1, 4):
            for cc in x_send(s, k):
                cc.start()

        @pl.when(s > 0)
        def _():
            second(s - 1)

        return carry

    lax.fori_loop(0, 4, step, 0)

    tail_norm(dn, xh, rstd, gain_ref, back, qkvc)
    second(3)
    tail_put(order_ref, qkvc, dtok_ref)

    def collect(s, carry):
        hp = hp_of(s)
        total = zs[s, z].astype(f32)
        for k in range(1, 8):
            z_send(s, k).wait_recv()
            total = total + zr[s, k - 1].astype(f32)
        for k in range(3):
            at = pl.ds(pl.multiple_of(512 * k + hp * 128, 128), 128)
            mq[:, at] = total[:, 128 * k : 128 * k + 128] + errq_ref[:, at]
        return carry

    lax.fori_loop(0, 4, collect, 0)
    for k in range(1, 8):
        zo_send(0, 0, k).wait_recv()
    so = dy_of((y - z // 2 + 4) % 4)
    total = zso[so, z % 2].astype(f32)
    for k in range(7):
        total = total + zro[k].astype(f32)
    mo[...] = total + erro_ref[...]

    mqv = mq[...]
    mov = mo[...]
    bqi = jnp.concatenate([qq_ref[...].astype(f32), jnp.zeros((96, 1536), f32)], 0).astype(bf16)
    boi = jnp.concatenate(
        [jnp.zeros((32, 512), f32), qo_ref[...].astype(f32), jnp.zeros((64, 512), f32)], 0
    ).astype(bf16)
    part = dnt(split3(mqv), bqi) + dnt(split3(mov), boi)
    lr[r] = ((part[0:16] + part[16:32]) + part[32:48]) * (1.0 / 127.0)
    for k in range(1, 8):
        remote(lr.at[r], lr.at[r], l_s.at[k - 1], l_r.at[k - 1], rp(k)).start()
    for k in range(1, 8):
        src = (r - k + 8) % 8
        remote(lr.at[src], lr.at[src], l_s.at[k - 1], l_r.at[k - 1], rp(k)).wait_recv()
    left = lr[0]
    for k in range(1, 8):
        left = left + lr[k]
    left = left * 0.125

    lt = left.T
    lane = lax.broadcasted_iota(jnp.int32, (32, 128), 1)
    full = hdot(lt, left)
    gx[x] = jnp.where(lane < 32, full[0:32], jnp.where(lane < 64, full[32:64], 0.0))
    for k in range(1, 4):
        remote(gx.at[x], gx.at[x], gx_s.at[k - 1], gx_r.at[k - 1], xp(k)).start()
    tq = hdot(lt[0:32], mqv)
    to = hdot(lt[32:64], mov)
    for k in range(12):
        tb[k] = tq[:, 128 * k : 128 * k + 128]
    for k in range(4):
        tb[12 + k] = to[:, 128 * k : 128 * k + 128]
    e1 = remote(tb.at[pl.ds(8 * (1 - c), 8)], er1, e_s.at[0, 0], e_r.at[0, 0], cp)
    e1.start()
    for k in range(1, 4):
        src = (x - k + 4) % 4
        remote(gx.at[src], gx.at[src], gx_s.at[k - 1], gx_r.at[k - 1], xp(k)).wait_recv()
    gz[z] = (gx[0] + gx[1]) + (gx[2] + gx[3])
    for k in range(1, 8):
        remote(gz.at[z], gz.at[z], gz_s.at[k - 1], gz_r.at[k - 1], zp(k)).start()
    e1.wait_recv()
    t1[...] = (tb[pl.ds(8 * c, 8)] + er1[...]).reshape(4, 2, 32, 128)
    e2 = [
        remote(t1.at[(x + k) % 4], ex.at[k - 1], e_s.at[1, k - 1], e_r.at[1, k - 1], xp(k))
        for k in range(1, 4)
    ]
    for cc in e2:
        cc.start()
    for cc in e2:
        cc.wait_recv()
    t2[...] = ((t1[x] + ex[0]) + (ex[1] + ex[2])).reshape(4, 16, 128)
    e3 = [
        remote(t2.at[(y + k) % 4], ey.at[k - 1], e_s.at[2, k - 1], e_r.at[2, k - 1], yp(k))
        for k in range(1, 4)
    ]
    for cc in e3:
        cc.start()
    for cc in e3:
        cc.wait_recv()
    ez[z] = (t2[y] + ey[0]) + (ey[1] + ey[2])
    for k in range(1, 8):
        remote(ez.at[z], ez.at[z], e_s.at[3, k - 1], e_r.at[3, k - 1], zp(k)).start()
    for k in range(1, 8):
        src = (z - k + 8) % 8
        remote(gz.at[src], gz.at[src], gz_s.at[k - 1], gz_r.at[k - 1], zp(k)).wait_recv()
    gram = gz[0]
    for k in range(1, 8):
        gram = gram + gz[k]
    iq, io = inverse_factors(gram)
    ortho_q = dnt_hi(left[:, 0:32], iq)
    ortho_o = dnt_hi(left[:, 32:64], io)
    for k in range(1, 8):
        src = (z - k + 8) % 8
        remote(ez.at[src], ez.at[src], e_s.at[3, k - 1], e_r.at[3, k - 1], zp(k)).wait_recv()
    t4 = ez[0]
    for k in range(1, 8):
        t4 = t4 + ez[k]
    R[c, x, y] = t4
    for k in range(1, 4):
        remote(R.at[c, x, y], R.at[c, x, y], e_s.at[4, k - 1], e_r.at[4, k - 1], yp(k)).start()
    for k in range(1, 4):
        src = (y - k + 4) % 4
        remote(R.at[c, x, src], R.at[c, x, src], e_s.at[4, k - 1], e_r.at[4, k - 1], yp(k)).wait_recv()
    for k in range(1, 4):
        remote(R.at[c, x], R.at[c, x], e_s.at[5, k - 1], e_r.at[5, k - 1], xp(k)).start()
    for k in range(1, 4):
        src = (x - k + 4) % 4
        remote(R.at[c, src], R.at[c, src], e_s.at[5, k - 1], e_r.at[5, k - 1], xp(k)).wait_recv()
    remote(R.at[c], R.at[c], e_s.at[6, 0], e_r.at[6, 0], cp).start()
    remote(R.at[1 - c], R.at[1 - c], e_s.at[6, 0], e_r.at[6, 0], cp).wait_recv()

    blocks = R[...].reshape(16, 32, 128)
    right_q = hdot(iq, jnp.concatenate([blocks[k] for k in range(12)], 1)) * 0.125
    right_o = hdot(io, jnp.concatenate([blocks[12 + k] for k in range(4)], 1)) * 0.125
    bq_ref[...] = right_q
    bo_ref[...] = right_o
    grad_q = hdot(ortho_q, right_q)
    grad_o = hdot(ortho_o, right_o)
    gradq_ref[...] = grad_q
    grado_ref[...] = grad_o
    nerrq_ref[...] = mqv - grad_q
    nerro_ref[...] = mov - grad_o

    @pl.when(source)
    def _():
        for k in range(1, 8):
            remote(W.at[y, z, x], W.at[y, z, x], az_s.at[0, k - 1], az_r.at[0, k - 1], zp(k)).wait_send()

        @pl.when((z // 2) == y)
        def _():
            for k in range(1, 8):
                remote(WO.at[z, x], WO.at[z, x], az_s.at[1, k - 1], az_r.at[1, k - 1], zp(k)).wait_send()

        for k in range(1, 4):
            remote(W.at[y, :, x], W.at[y, :, x], ax_s.at[0, k - 1], ax_r.at[0, k - 1], xp(k)).wait_send()
            o = WO.at[pl.ds(2 * y, 2), x]
            remote(o, o, ax_s.at[1, k - 1], ax_r.at[1, k - 1], xp(k)).wait_send()

    for dy in (1, 3, 2):
        for cc in y_copy(dy, y):
            cc.wait_send()

    def sent(s, carry):
        for cc in core_copy(s, c):
            cc.wait_send()
        for k in range(1, 4):
            for cc in x_send(s, k):
                cc.wait_send()
        for k in range(1, 8):
            z_send(s, k).wait_send()
        zo_each(s, lambda cc: cc.wait_send())
        return carry

    lax.fori_loop(0, 4, sent, 0)
    for k in range(1, 8):
        remote(lr.at[r], lr.at[r], l_s.at[k - 1], l_r.at[k - 1], rp(k)).wait_send()
        remote(gz.at[z], gz.at[z], gz_s.at[k - 1], gz_r.at[k - 1], zp(k)).wait_send()
        remote(ez.at[z], ez.at[z], e_s.at[3, k - 1], e_r.at[3, k - 1], zp(k)).wait_send()
    e1.wait_send()
    for k in range(1, 4):
        remote(gx.at[x], gx.at[x], gx_s.at[k - 1], gx_r.at[k - 1], xp(k)).wait_send()
        e2[k - 1].wait_send()
        e3[k - 1].wait_send()
        remote(R.at[c, x, y], R.at[c, x, y], e_s.at[4, k - 1], e_r.at[4, k - 1], yp(k)).wait_send()
        remote(R.at[c, x], R.at[c, x], e_s.at[5, k - 1], e_r.at[5, k - 1], xp(k)).wait_send()
    remote(R.at[c], R.at[c], e_s.at[6, 0], e_r.at[6, 0], cp).wait_send()


def per_device(tokens, cotangent, window_order, gain, w_qkv, w_out, err_qkv, err_out, q_qkv, q_out):
    scale = float(lax.axis_size("fsdp") * tokens.shape[0]) ** (-0.5)
    vmem = pl.BlockSpec(memory_space=pltpu.VMEM)
    V = pltpu.VMEM
    dma = pltpu.SemaphoreType.DMA
    outs = pl.pallas_call(
        functools.partial(kernel, scale),
        out_shape=(
            jax.ShapeDtypeStruct((576, 512), bf16),
            jax.ShapeDtypeStruct((16, 1536), f32),
            jax.ShapeDtypeStruct((16, 512), f32),
            jax.ShapeDtypeStruct((16, 1536), f32),
            jax.ShapeDtypeStruct((16, 512), f32),
            jax.ShapeDtypeStruct((32, 1536), f32),
            jax.ShapeDtypeStruct((32, 512), f32),
        ),
        in_specs=[vmem] * 10,
        out_specs=(vmem,) * 7,
        scratch_shapes=[
            V((4, 8, 4, 16, 384), bf16), V((8, 4, 16, 512), bf16),
            V((576, 512), bf16), V((576, 512), bf16), V((512, 576), bf16),
            V((576, 512), f32), V((576, 1), f32), V((576, 384), bf16), V((576, 512), f32), V((576, 512), bf16),
            V((4, 8, 4, 16, 384), bf16), V((4, 3, 8, 16, 384), bf16), V((4, 8, 16, 384), bf16), V((4, 7, 16, 384), bf16),
            V((4, 2, 4, 16, 512), bf16), V((4, 3, 2, 16, 512), bf16), V((4, 2, 16, 512), bf16), V((7, 16, 512), bf16),
            V((16, 1536), f32), V((16, 512), f32),
            V((8, 16, 128), f32), V((4, 32, 128), f32), V((8, 32, 128), f32),
            V((16, 32, 128), f32), V((8, 32, 128), f32), V((4, 2, 32, 128), f32), V((3, 2, 32, 128), f32),
            V((4, 16, 128), f32), V((3, 16, 128), f32), V((8, 16, 128), f32), V((2, 4, 4, 16, 128), f32),
            dma((2, 7)), dma((2, 7)), dma((2, 3)), dma((2, 3)), dma((2, 3)), dma((2, 3)), dma((2, 4)), dma((2, 4)),
            dma((2, 4, 3)), dma((2, 4, 3)), dma((1, 4, 7)), dma((2, 4, 7)), dma((4, 2)),
            dma((7,)), dma((7,)), dma((3,)), dma((3,)), dma((7,)), dma((7,)), dma((7, 7)), dma((7, 7)),
        ],
        compiler_params=pltpu.CompilerParams(
            collective_id=0, has_side_effects=True, vmem_limit_bytes=48 * 2**20
        ),
    )(
        window_order, tokens, cotangent, gain.reshape(1, 512), w_qkv, w_out,
        err_qkv.reshape(16, 1536), err_out.reshape(16, 512), q_qkv.T, q_out.T,
    )
    dt, gq, go, eq, eo, bq, bo = outs
    return dt, gq, go, eq[None], eo[None], bq.T, bo.T


def solution(mesh):
    return jax.shard_map(
        per_device,
        mesh=mesh,
        in_specs=(
            P(("rep", "fsdp"), None),
            P(("rep", "fsdp"), None),
            P(("rep", "fsdp"), None),
            P(),
            P("fsdp", None),
            P("fsdp", None),
            P("rep", "fsdp", None),
            P("rep", "fsdp", None),
            P(),
            P(),
        ),
        out_specs=(
            P(("rep", "fsdp"), None),
            P("fsdp", None),
            P("fsdp", None),
            P("rep", "fsdp", None),
            P("rep", "fsdp", None),
            P(),
            P(),
        ),
        check_vma=False,
    )
```

```python
import functools

import jax
import jax.numpy as jnp
from jax import lax
from jax.experimental import pallas as pl
from jax.experimental.pallas import tpu as pltpu
from jax.sharding import PartitionSpec as P

f32 = jnp.float32
bf16 = jnp.bfloat16
MESH = pl.DeviceIdType.MESH
def dot(a,b): return jnp.dot(a,b,preferred_element_type=f32)
def dnt(a,b): return lax.dot_general(a,b,(((1,),(1,)),((),())),preferred_element_type=f32)
WT=144; NW=4
LOG2E=1.4426950408889634
def front_window(w,order_ref,tok_ref,cot_ref,gain_ref,back_ref,n_ref,xh_ref,rstd_ref):
        row=order_ref[...]
        T=row.shape[1]
        gain=gain_ref[...]
        sl=pl.ds(w*WT,WT)
        si=lax.broadcasted_iota(jnp.int32,(WT,T),0)+w*WT
        li=lax.broadcasted_iota(jnp.int32,(WT,T),1)
        col=jnp.sum(jnp.where(si==li,row,0).astype(f32),axis=1,keepdims=True).astype(jnp.int32)
        oh=jnp.where(col==li,1.0,0.0).astype(bf16)
        x=dot(oh,tok_ref[...])
        back_ref[sl,:]=dot(oh,cot_ref[...]).astype(bf16)
        ce=x-jnp.mean(x,-1,keepdims=True)
        rs=lax.rsqrt(jnp.mean(ce*ce,-1,keepdims=True)+1e-5)
        xh=ce*rs
        xh_ref[sl,:]=xh
        rstd_ref[sl,:]=rs
        n=(xh*gain).astype(bf16)
        n_ref[sl,:]=n
def pair(n_ref,nt_ref,back_ref,W,WO,d_ref,dn_ref,qkvc_ref,scale,first,g_store,go_store,mid=None):
    qkvc_ref[:,:384]=dot(n_ref[...],W).astype(bf16)
    qkvc_ref[:,384:]=dnt(back_ref[...],WO).astype(bf16)
    if mid is not None: mid()
    lane=lax.broadcasted_iota(jnp.int32,(WT,128),1)
    go=jnp.zeros((128,512),f32)
    for w in range(NW):
        sl=pl.ds(w*WT,WT)
        q=qkvc_ref[sl,0:128]; k=qkvc_ref[sl,128:256]; v=qkvc_ref[sl,256:384]; c=qkvc_ref[sl,384:512]
        qt=q.T; kt=k.T; vt=v.T; ct=c.T
        cts=[];dqs=[]
        dv=jnp.zeros((WT,128),f32); dk=jnp.zeros((WT,128),f32)
        for h in range(2):
            m=(lane<64) if h==0 else (lane>=64)
            z=jnp.zeros((),bf16)
            s=dot(jnp.where(m,k,z),qt)
            mx=jnp.max(s,axis=0,keepdims=True)
            e=jnp.exp2((s-mx)*(0.125*LOG2E))
            wt=e*(1.0/jnp.sum(e,axis=0,keepdims=True))
            p=wt.astype(bf16)
            cts.append(dot(vt[64*h:64*h+64],p))
            dp=dot(jnp.where(m,v,z),ct).astype(bf16).astype(f32)
            t=wt*dp
            ds=(t-wt*jnp.sum(t,axis=0,keepdims=True)).astype(bf16)
            dv=dv+dot(p,jnp.where(m,c,z))
            dk=dk+dot(ds,jnp.where(m,q,z))
            dqs.append(dot(kt[64*h:64*h+64],ds))
        ctx=jnp.concatenate(cts,0).astype(bf16)
        go=go+dot(ctx,back_ref[sl,:])
        dq=(jnp.concatenate(dqs,0)*0.125).astype(bf16).T
        d_ref[sl,0:128]=dq
        d_ref[sl,128:256]=(dk*0.125).astype(bf16)
        d_ref[sl,256:384]=dv.astype(bf16)
    go_store((go*scale).astype(bf16))
    g_store((dot(nt_ref[...],d_ref[...])*scale).astype(bf16))
    dn=dnt(d_ref[...],W)
    dn_ref[...]=jnp.where(first,0.0,dn_ref[...])+dn
def tail_norm(dn_ref,xh_ref,rstd_ref,gain_ref,back_ref,dwin_ref):
    gain=gain_ref[...]
    for w in range(NW):
        sl=pl.ds(w*WT,WT)
        dx=dn_ref[sl,:].astype(bf16).astype(f32)*gain
        xh=xh_ref[sl,:]
        d=rstd_ref[sl,:]*(dx-jnp.mean(dx,-1,keepdims=True)-xh*jnp.mean(dx*xh,-1,keepdims=True))
        dwin_ref[sl,:]=(back_ref[sl,:].astype(f32)+d).astype(bf16)

def tail_put(order_ref,dwin_ref,out_ref):
    row=order_ref[...]
    T=row.shape[1]
    for w in range(NW):
        sl=pl.ds(w*WT,WT)
        si=lax.broadcasted_iota(jnp.int32,(WT,T),0)+w*WT
        oh=jnp.where(si==row,1.0,0.0).astype(bf16)
        out_ref[sl,:]=dot(oh,dwin_ref[...]).astype(bf16)


def remote(src, dst, ss, rs, dev):
    return pltpu.make_async_remote_copy(
        src_ref=src, dst_ref=dst, send_sem=ss, recv_sem=rs, device_id=dev, device_id_type=MESH
    )


def split3(v):
    a = v.astype(bf16)
    r = v - a.astype(f32)
    b = r.astype(bf16)
    c = (r - b.astype(f32)).astype(bf16)
    return jnp.concatenate([a, b, c], 0)


def pieces(v):
    a = v.astype(bf16)
    r = v - a.astype(f32)
    b = r.astype(bf16)
    return a, b, (r - b.astype(f32)).astype(bf16)


def hdot(a, b):
    rows = a.shape[0]
    b1, b2, b3 = pieces(b)
    a3 = split3(a)
    u = dot(a3, b1)
    v = dot(a3[: 2 * rows], b2)
    w = dot(a3[:rows], b3)
    return u[:rows] + ((u[rows : 2 * rows] + v[:rows]) + (u[2 * rows :] + (v[rows:] + w)))


def inverse_factors(gram):
    lane = lax.broadcasted_iota(jnp.int32, (32, 128), 1)
    row = lax.broadcasted_iota(jnp.int32, (32, 128), 0)
    first = (lane % 64) < 32
    state = jnp.where(lane < 64, gram, jnp.where((lane % 32) == row, 1.0, 0.0))
    for j in range(31):
        cols = jnp.where(first, state[:, j : j + 1], state[:, 32 + j : 33 + j])
        factor = cols / cols[j : j + 1, :]
        state = state - jnp.where(row > j, factor, 0.0) * state[j : j + 1, :]
    out = []
    for k in range(2):
        diag = jnp.sum(jnp.where(lane == row + 32 * k, state, 0.0), axis=1, keepdims=True)
        out.append(state[:, 64 + 32 * k : 96 + 32 * k] * (1.0 / jnp.sqrt(diag)))
    return out


def kernel(
    scale,
    order_in, tok_in, cot_in, gain_in, w_in, wo_in, errq_in, erro_in, qq_in, qo_in,
    dtok_ref, R, left_ref, inv_ref, mq, mo,
    order_ref, tok_ref, cot_ref, gain_ref, w_ref, wo_ref, errq_ref, erro_ref, qq_ref, qo_ref, in_sem,
    W, WO, back, n, nt, xh, rstd, d, dn, qkvc,
    gbuf, xr, xm, zs, zr, gobuf, xro, xmo, zso, zro,
    lr, mb, mr, t1, ex, ez,
    az_s, az_r, ax_s, ax_r, ay_s, ay_r, ac_s, ac_r,
    rx_s, rx_r, rz_s, rz_r, ro_s,
    l_s, l_r, e_s, e_r,
):
    r = lax.axis_index("rep")
    f = lax.axis_index("fsdp")
    y = r // 2
    c = r % 2
    z = f // 4
    x = f % 4

    def zp(dz):
        return (r, ((z + dz) % 8) * 4 + x)

    def xp(dx):
        return (r, z * 4 + (x + dx) % 4)

    def yp(dy):
        return (((y + dy) % 4) * 2 + c, f)

    cp = (y * 2 + 1 - c, f)

    def rp(k):
        return ((r + k) % 8, f)

    loads = [
        pltpu.make_async_copy(a, b, in_sem.at[k])
        for k, (a, b) in enumerate(
            (
                (w_in, w_ref), (wo_in, wo_ref), (order_in, order_ref), (gain_in, gain_ref), (tok_in, tok_ref),
                (cot_in, cot_ref), (errq_in, errq_ref), (erro_in, erro_ref), (qq_in, qq_ref), (qo_in, qo_ref),
            )
        )
    ]
    for cc in loads:
        cc.start()
    barrier = pltpu.get_barrier_semaphore()
    for k in range(1, 8):
        pl.semaphore_signal(barrier, inc=1, device_id=zp(k), device_id_type=MESH)
        pl.semaphore_signal(barrier, inc=1, device_id=rp(k), device_id_type=MESH)
    for k in range(1, 4):
        pl.semaphore_signal(barrier, inc=1, device_id=xp(k), device_id_type=MESH)

    def fr(w):
        front_window(w, order_ref, tok_ref, cot_ref, gain_ref, back, n, xh, rstd)

    source = (x // 2) == c
    for cc in loads[:6]:
        cc.wait()

    own = y % 2

    @pl.when(source)
    def _():
        for i in range(2):
            for k in range(3):
                W[2 * own + i, z, x, :, 128 * k : 128 * k + 128] = w_ref[
                    :, pl.ds(pl.multiple_of(512 * k + (2 * own + i) * 128, 128), 128)
                ]

        @pl.when((z // 4) == own)
        def _():
            WO[z, x] = wo_ref[...]

    fr(0)
    pl.semaphore_wait(barrier, 17)

    def w_z(i, k, at):
        a = W.at[2 * own + i, at, x]
        return remote(a, a, az_s.at[i, k - 1], az_r.at[i, k - 1], zp(k))

    def wo_z(k, at):
        a = WO.at[at, x]
        return remote(a, a, az_s.at[2, k - 1], az_r.at[2, k - 1], zp(k))

    def w_x(i, k, at):
        a = W.at[2 * own + i, :, at]
        b = WO.at[pl.ds(2 * (2 * own + i), 2), at]
        return (
            remote(a, a, ax_s.at[0, i, k - 1], ax_r.at[0, i, k - 1], xp(k)),
            remote(b, b, ax_s.at[1, i, k - 1], ax_r.at[1, i, k - 1], xp(k)),
        )

    def wait_x(i):
        for k in range(1, 4):
            src = (x - k + 4) % 4

            @pl.when((src // 2) == c)
            def _():
                for cc in w_x(i, k, src):
                    cc.wait_recv()

    @pl.when(source)
    def _():
        for i in range(2):
            for k in range(1, 8):
                w_z(i, k, z).start()
            if i == 0:

                @pl.when((z // 4) == own)
                def _():
                    for k in range(1, 8):
                        wo_z(k, z).start()

    fr(1)
    fr(2)

    @pl.when(source)
    def _():
        for i in range(2):
            for k in range(1, 8):
                src = (z - k + 8) % 8
                w_z(i, k, src).wait_recv()

                @pl.when((src // 2) == 2 * own + i)
                def _():
                    wo_z(k, src).wait_recv()

            for k in range(1, 4):
                for cc in w_x(i, k, x):
                    cc.start()

    fr(3)
    nt[...] = n[...].T

    def hp_of(s):
        return (2 * own + s) % 4

    def half(hp, core):
        return W.at[hp, :, pl.ds(2 * core, 2)], WO.at[pl.ds(2 * hp, 2), pl.ds(2 * core, 2)]

    def core_copy(s, core):
        a, b = half(hp_of(s), core)
        return (
            remote(a, a, ac_s.at[0, s], ac_r.at[0, s], cp),
            remote(b, b, ac_s.at[1, s], ac_r.at[1, s], cp),
        )

    def y_copy(i, hp):
        a, b = half(hp, c)
        to = yp((1 + 2 * own + 2 * i) % 4)
        return (
            remote(a, a, ay_s.at[0, i], ay_r.at[0, i], to),
            remote(b, b, ay_s.at[1, i], ay_r.at[1, i], to),
        )

    def spread(i):
        wait_x(i)
        for cc in y_copy(i, 2 * own + i):
            cc.start()
        for cc in core_copy(i, c):
            cc.start()

    spread(0)

    def x_copy(kind, s, way):
        to = xp(1 + 2 * way)
        h = 1 - way if kind == 1 else way
        if kind == 2:
            a, b = xm.at[s, way], xmo.at[s, pl.ds(way, 1)]
        else:
            at = (x + 2) % 4 if kind == 0 else (x + 1 + 2 * way) % 4
            a, b = gbuf.at[s, pl.ds(4 * h, 4), at], gobuf.at[s, pl.ds(h, 1), at]
        return (
            remote(a, xr.at[kind, s, way], rx_s.at[0, kind, s, way], rx_r.at[0, kind, s, way], to),
            remote(b, xro.at[kind, s, pl.ds(way, 1)], rx_s.at[1, kind, s, way], rx_r.at[1, kind, s, way], to),
        )

    def merge(s):
        for way in range(2):
            for cc in x_copy(0, s, way):
                cc.wait_recv()
            at = (x + 1 + 2 * way) % 4
            xm[s, way] = (gbuf[s, 4 * way : 4 * way + 4, at].astype(f32) + xr[0, s, way].astype(f32)).astype(bf16)
            xmo[s, way] = (gobuf[s, way, at].astype(f32) + xro[0, s, way].astype(f32)).astype(bf16)
            for cc in x_copy(2, s, way):
                cc.start()

    def z_send(s, k):
        return remote(
            zs.at[s, (z + k) % 8], zr.at[s, k - 1], rz_s.at[0, s, k - 1], rz_r.at[0, s, k - 1], zp(k)
        )

    def zo_send(s, j, k):
        return remote(zso.at[s, j], zro.at[k - 1], ro_s.at[s, j], rz_r.at[1, 0, k - 1], zp(k))

    def zo_each(s, act):
        for j in range(2):
            k = (2 * hp_of(s) + j - z + 8) % 8

            @pl.when(k > 0)
            def _():
                act(zo_send(s, j, k))

    def second(s):
        for kind in (1, 2):
            for way in range(2):
                for cc in x_copy(kind, s, way):
                    cc.wait_recv()
        for h in range(2):
            rows = slice(4 * h, 4 * h + 4)
            total = gbuf[s, rows, x].astype(f32) + (xr[1, s, 1 - h].astype(f32) + xr[2, s, h].astype(f32))
            zs[s, rows] = total.astype(bf16)
            total = gobuf[s, h, x].astype(f32) + (xro[1, s, 1 - h].astype(f32) + xro[2, s, h].astype(f32))
            zso[s, h] = total.astype(bf16)
        for k in range(1, 8):
            z_send(s, k).start()
        zo_each(s, lambda cc: cc.start())

    def step(s, carry):
        hp = hp_of(s)
        for cc in core_copy(s, 1 - c):
            cc.wait_recv()

        def mid():
            @pl.when(s == 0)
            def _():
                spread(1)

            @pl.when((s == 1) | (s == 2))
            def _():
                for cc in y_copy(s - 1, hp_of(s + 1)):
                    cc.wait_recv()
                for cc in core_copy(s + 1, c):
                    cc.start()

        def g_store(v):
            gbuf[s] = v.reshape(8, 4, 16, 384)

        def go_store(v):
            gobuf[s] = v.reshape(2, 4, 16, 512)

        pair(
            n, nt, back, W[hp].reshape(512, 384), WO[pl.ds(2 * hp, 2)].reshape(128, 512),
            d, dn, qkvc, scale, s == 0, g_store, go_store, mid,
        )
        for kind in (0, 1):
            for way in range(2):
                for cc in x_copy(kind, s, way):
                    cc.start()

        @pl.when(s > 0)
        def _():
            merge(s - 1)

        @pl.when(s > 1)
        def _():
            second(s - 2)

        return carry

    lax.fori_loop(0, 4, step, 0)

    tail_norm(dn, xh, rstd, gain_ref, back, qkvc)
    merge(3)
    second(2)
    tail_put(order_ref, qkvc, dtok_ref)
    second(3)

    for cc in loads[6:]:
        cc.wait()

    def collect(s, carry):
        hp = hp_of(s)
        total = zs[s, z].astype(f32)
        for k in range(1, 8):
            z_send(s, k).wait_recv()
            total = total + zr[s, k - 1].astype(f32)
        for k in range(3):
            at = pl.ds(pl.multiple_of(512 * k + hp * 128, 128), 128)
            mq[:, at] = total[:, 128 * k : 128 * k + 128] + errq_ref[:, at]
        return carry

    lax.fori_loop(0, 4, collect, 0)
    for k in range(1, 8):
        zo_send(0, 0, k).wait_recv()
    so = (z // 2 - 2 * own + 4) % 4
    total = zso[so, z % 2].astype(f32)
    for k in range(7):
        total = total + zro[k].astype(f32)
    mo[...] = total + erro_ref[...]

    mqv = mq[...]
    mov = mo[...]
    for k in range(12):
        mb[k // 2, k % 2] = mqv[:, 128 * k : 128 * k + 128]
    for k in range(4):
        mb[6 + k // 2, k % 2] = mov[:, 128 * k : 128 * k + 128]

    def m_copy(k):
        return remote(mb.at[(r + k) % 8], mr.at[k - 1], l_s.at[1, k - 1], l_r.at[1, k - 1], rp(k))

    def l_copy(k, at):
        return remote(lr.at[at], lr.at[at], l_s.at[0, k - 1], l_r.at[0, k - 1], rp(k))

    for k in range(1, 8):
        m_copy(k).start()
    bqi = jnp.concatenate([qq_ref[...].astype(f32), jnp.zeros((96, 1536), f32)], 0).astype(bf16)
    boi = jnp.concatenate(
        [jnp.zeros((32, 512), f32), qo_ref[...].astype(f32), jnp.zeros((64, 512), f32)], 0
    ).astype(bf16)
    part = dnt(split3(mqv), bqi) + dnt(split3(mov), boi)
    lr[r] = ((part[0:16] + part[16:32]) + part[32:48]) * (1.0 / 127.0)
    for k in range(1, 8):
        l_copy(k, r).start()
    for k in range(1, 8):
        m_copy(k).wait_recv()
    total = mb[r]
    for k in range(7):
        total = total + mr[k]
    for k in range(1, 8):
        l_copy(k, (r - k + 8) % 8).wait_recv()
    left = lr[0]
    for k in range(1, 8):
        left = left + lr[k]
    left = left * 0.125
    left_ref[...] = left

    lt = left.T
    lane = lax.broadcasted_iota(jnp.int32, (32, 128), 1)
    full = hdot(lt, left)
    gram = jnp.where(lane < 32, full[0:32], jnp.where(lane < 64, full[32:64], 0.0))
    mine = jnp.where(r < 6, lt[0:32], lt[32:64])
    for j in range(2):
        t = hdot(mine, total[j])
        t1[2 * j, 0:16] = t[0:16]
        t1[2 * j + 1, 0:16] = t[16:32]
    for k in range(4):
        t1[k, 16:48] = gram
    ex[x] = t1[x]

    def e_x(k, to, at):
        return remote(t1.at[to], ex.at[at], e_s.at[0, k - 1], e_r.at[0, k - 1], xp(k))

    def e_z(k, at):
        return remote(ez.at[at], ez.at[at], e_s.at[1, k - 1], e_r.at[1, k - 1], zp(k))

    def a_x(k, at):
        return remote(R.at[r, at], R.at[r, at], e_s.at[2, k - 1], e_r.at[2, k - 1], xp(k))

    def a_r(k, at):
        return remote(R.at[at], R.at[at], e_s.at[3, k - 1], e_r.at[3, k - 1], rp(k))

    for k in range(1, 4):
        e_x(k, (x + k) % 4, x).start()
    for k in range(1, 4):
        e_x(k, x, (x - k + 4) % 4).wait_recv()
    ez[z] = (ex[0] + ex[1]) + (ex[2] + ex[3])
    for k in range(1, 8):
        e_z(k, z).start()
    for k in range(1, 8):
        e_z(k, (z - k + 8) % 8).wait_recv()
    total = ez[0]
    for k in range(1, 8):
        total = total + ez[k]
    R[r, x] = total[0:16]
    for k in range(1, 4):
        a_x(k, x).start()
    iq, io = inverse_factors(total[16:48])
    inv_ref[0] = iq
    inv_ref[1] = io
    for k in range(1, 4):
        a_x(k, (x - k + 4) % 4).wait_recv()
    for k in range(1, 8):
        a_r(k, r).start()
    for k in range(1, 8):
        a_r(k, (r - k + 8) % 8).wait_recv()

    @pl.when(source)
    def _():
        for i in range(2):
            for k in range(1, 8):
                w_z(i, k, z).wait_send()
            for k in range(1, 4):
                for cc in w_x(i, k, x):
                    cc.wait_send()

        @pl.when((z // 4) == own)
        def _():
            for k in range(1, 8):
                wo_z(k, z).wait_send()

    for i in range(2):
        for cc in y_copy(i, 2 * own + i):
            cc.wait_send()

    def sent(s, carry):
        for cc in core_copy(s, c):
            cc.wait_send()
        for kind in range(3):
            for way in range(2):
                for cc in x_copy(kind, s, way):
                    cc.wait_send()
        for k in range(1, 8):
            z_send(s, k).wait_send()
        zo_each(s, lambda cc: cc.wait_send())
        return carry

    lax.fori_loop(0, 4, sent, 0)
    for k in range(1, 8):
        m_copy(k).wait_send()
        l_copy(k, r).wait_send()
        e_z(k, z).wait_send()
        a_r(k, r).wait_send()
    for k in range(1, 4):
        e_x(k, (x + k) % 4, x).wait_send()
        a_x(k, x).wait_send()


def finish(
    dtok_in, R, left_ref, inv_ref, mq_ref, mo_ref,
    dtok_out, gradq_out, grado_out, nerrq_out, nerro_out, bq_out, bo_out,
    gradq, grado, nerrq, nerro, bq, bo, sem,
):
    def out(k, a, b):
        cc = pltpu.make_async_copy(a, b, sem.at[k])
        cc.start()
        return cc

    outs = [out(0, dtok_in, dtok_out)]
    left = left_ref[...]
    iq = inv_ref[0]
    io = inv_ref[1]
    ortho_q = hdot(left[:, 0:32], iq.T)
    ortho_o = hdot(left[:, 32:64], io.T)
    blocks = R[...].reshape(16, 32, 128)
    bq[...] = hdot(iq, jnp.concatenate([blocks[k] for k in range(12)], 1)) * 0.125
    outs.append(out(1, bq, bq_out))
    bo[...] = hdot(io, jnp.concatenate([blocks[12 + k] for k in range(4)], 1)) * 0.125
    outs.append(out(2, bo, bo_out))
    grad = hdot(ortho_q, bq[...])
    gradq[...] = grad
    nerrq[...] = mq_ref[...] - grad
    outs.append(out(3, gradq, gradq_out))
    outs.append(out(4, nerrq, nerrq_out))
    grad = hdot(ortho_o, bo[...])
    grado[...] = grad
    nerro[...] = mo_ref[...] - grad
    outs.append(out(5, grado, grado_out))
    outs.append(out(6, nerro, nerro_out))
    for cc in outs:
        cc.wait()


def per_device(tokens, cotangent, window_order, gain, w_qkv, w_out, err_qkv, err_out, q_qkv, q_out):
    scale = float(lax.axis_size("fsdp") * tokens.shape[0]) ** (-0.5)
    vmem = pl.BlockSpec(memory_space=pltpu.VMEM)
    V = pltpu.VMEM
    dma = pltpu.SemaphoreType.DMA
    hbm = pl.BlockSpec(memory_space=pl.ANY)

    def shape(dims, kind=f32):
        return jax.ShapeDtypeStruct(dims, kind)

    mid = pl.pallas_call(
        functools.partial(kernel, scale),
        out_shape=(
            shape((576, 512), bf16), shape((8, 4, 16, 128)), shape((16, 128)), shape((2, 32, 32)),
            shape((16, 1536)), shape((16, 512)),
        ),
        in_specs=[hbm] * 10,
        out_specs=(vmem,) * 6,
        scratch_shapes=[
            V((1, 576), jnp.int32), V((576, 512), bf16), V((576, 512), bf16), V((1, 512), f32),
            V((16, 1536), bf16), V((16, 512), bf16), V((16, 1536), f32), V((16, 512), f32),
            V((32, 1536), jnp.int32), V((32, 512), jnp.int32), dma((10,)),
            V((4, 8, 4, 16, 384), bf16), V((8, 4, 16, 512), bf16),
            V((576, 512), bf16), V((576, 512), bf16), V((512, 576), bf16),
            V((576, 512), f32), V((576, 1), f32), V((576, 384), bf16), V((576, 512), f32), V((576, 512), bf16),
            V((4, 8, 4, 16, 384), bf16), V((3, 4, 2, 4, 16, 384), bf16), V((4, 2, 4, 16, 384), bf16), V((4, 8, 16, 384), bf16), V((4, 7, 16, 384), bf16),
            V((4, 2, 4, 16, 512), bf16), V((3, 4, 2, 16, 512), bf16), V((4, 2, 16, 512), bf16), V((4, 2, 16, 512), bf16), V((7, 16, 512), bf16),
            V((8, 16, 128), f32), V((8, 2, 16, 128), f32), V((7, 2, 16, 128), f32),
            V((4, 48, 128), f32), V((4, 48, 128), f32), V((8, 48, 128), f32),
            dma((3, 7)), dma((3, 7)), dma((2, 2, 3)), dma((2, 2, 3)), dma((2, 2)), dma((2, 2)), dma((2, 4)), dma((2, 4)),
            dma((2, 3, 4, 2)), dma((2, 3, 4, 2)), dma((1, 4, 7)), dma((2, 4, 7)), dma((4, 2)),
            dma((2, 7)), dma((2, 7)), dma((4, 7)), dma((4, 7)),
        ],
        compiler_params=pltpu.CompilerParams(
            collective_id=0, has_side_effects=True, vmem_limit_bytes=56 * 2**20
        ),
    )(
        window_order, tokens, cotangent, gain.reshape(1, 512), w_qkv, w_out,
        err_qkv.reshape(16, 1536), err_out.reshape(16, 512), q_qkv.T, q_out.T,
    )
    dt, gq, go, eq, eo, bq, bo = pl.pallas_call(
        finish,
        out_shape=(
            shape((576, 512), bf16), shape((16, 1536)), shape((16, 512)), shape((16, 1536)), shape((16, 512)),
            shape((32, 1536)), shape((32, 512)),
        ),
        in_specs=[vmem] * 6,
        out_specs=(hbm,) * 7,
        scratch_shapes=[
            V((16, 1536), f32), V((16, 512), f32), V((16, 1536), f32), V((16, 512), f32),
            V((32, 1536), f32), V((32, 512), f32), dma((7,)),
        ],
    )(*mid)
    return dt, gq, go, eq[None], eo[None], bq.T, bo.T


def solution(mesh):
    return jax.shard_map(
        per_device,
        mesh=mesh,
        in_specs=(
            P(("rep", "fsdp"), None),
            P(("rep", "fsdp"), None),
            P(("rep", "fsdp"), None),
            P(),
            P("fsdp", None),
            P("fsdp", None),
            P("rep", "fsdp", None),
            P("rep", "fsdp", None),
            P(),
            P(),
        ),
        out_specs=(
            P(("rep", "fsdp"), None),
            P("fsdp", None),
            P("fsdp", None),
            P("rep", "fsdp", None),
            P("rep", "fsdp", None),
            P(),
            P(),
        ),
        check_vma=False,
    )
```

```python
import functools

import jax
import jax.numpy as jnp
from jax import lax
from jax.experimental import pallas as pl
from jax.experimental.pallas import tpu as pltpu
from jax.sharding import PartitionSpec as P

f32 = jnp.float32
bf16 = jnp.bfloat16
MESH = pl.DeviceIdType.MESH
def dot(a,b): return jnp.dot(a,b,preferred_element_type=f32)
def dnt(a,b): return lax.dot_general(a,b,(((1,),(1,)),((),())),preferred_element_type=f32)
WT=144; NW=4
LOG2E=1.4426950408889634
def front_window(w,order_ref,tok_ref,cot_ref,gain_ref,back_ref,n_ref,xh_ref,rstd_ref):
        row=order_ref[...]
        T=row.shape[1]
        gain=gain_ref[...]
        sl=pl.ds(w*WT,WT)
        si=lax.broadcasted_iota(jnp.int32,(WT,T),0)+w*WT
        li=lax.broadcasted_iota(jnp.int32,(WT,T),1)
        col=jnp.sum(jnp.where(si==li,row,0).astype(f32),axis=1,keepdims=True).astype(jnp.int32)
        oh=jnp.where(col==li,1.0,0.0).astype(bf16)
        x=dot(oh,tok_ref[...])
        back_ref[sl,:]=dot(oh,cot_ref[...]).astype(bf16)
        ce=x-jnp.mean(x,-1,keepdims=True)
        rs=lax.rsqrt(jnp.mean(ce*ce,-1,keepdims=True)+1e-5)
        xh=ce*rs
        xh_ref[sl,:]=xh
        rstd_ref[sl,:]=rs
        n=(xh*gain).astype(bf16)
        n_ref[sl,:]=n
def pair(n_ref,nt_ref,back_ref,W,WO,d_ref,dn_ref,qkvc_ref,scale,first,g_store,go_store,mid=None):
    qkvc_ref[:,:384]=dot(n_ref[...],W).astype(bf16)
    qkvc_ref[:,384:]=dnt(back_ref[...],WO).astype(bf16)
    if mid is not None: mid()
    lane=lax.broadcasted_iota(jnp.int32,(WT,128),1)
    go=jnp.zeros((128,512),f32)
    for w in range(NW):
        sl=pl.ds(w*WT,WT)
        q=qkvc_ref[sl,0:128]; k=qkvc_ref[sl,128:256]; v=qkvc_ref[sl,256:384]; c=qkvc_ref[sl,384:512]
        kt=k.T; vt=v.T
        cts=[];dqs=[]
        dv=jnp.zeros((WT,128),f32); dk=jnp.zeros((WT,128),f32)
        z=jnp.zeros((),bf16)
        lo=lane<64
        def two(a): return jnp.concatenate([jnp.where(lo,a,z),jnp.where(lo,z,a)],0)
        s2=dnt(two(k),q); d2=dnt(two(v),c)
        ps=[];dss=[]
        for h in range(2):
            s=s2[WT*h:WT*h+WT]
            mx=jnp.max(s,axis=0,keepdims=True)
            e=jnp.exp2((s-mx)*(0.125*LOG2E))
            wt=e*(1.0/jnp.sum(e,axis=0,keepdims=True))
            p=wt.astype(bf16)
            dp=d2[WT*h:WT*h+WT].astype(bf16).astype(f32)
            t=wt*dp
            ds=(t-wt*jnp.sum(t,axis=0,keepdims=True)).astype(bf16)
            ps.append(p);dss.append(ds)
            cts.append(dot(vt[64*h:64*h+64],p))
            dqs.append(dot(kt[64*h:64*h+64],ds))
        dv=jnp.where(lo,dot(ps[0],c),dot(ps[1],c))
        dk=jnp.where(lo,dot(dss[0],q),dot(dss[1],q))
        ctx=jnp.concatenate(cts,0).astype(bf16)
        go=go+dot(ctx,back_ref[sl,:])
        dq=(jnp.concatenate(dqs,0)*0.125).astype(bf16).T
        d_ref[sl,0:128]=dq
        d_ref[sl,128:256]=(dk*0.125).astype(bf16)
        d_ref[sl,256:384]=dv.astype(bf16)
    go_store((go*scale).astype(bf16))
    g_store((dot(nt_ref[...],d_ref[...])*scale).astype(bf16))
    dn=dnt(d_ref[...],W)
    dn_ref[...]=jnp.where(first,0.0,dn_ref[...])+dn
def tail_norm(dn_ref,xh_ref,rstd_ref,gain_ref,back_ref,dwin_ref):
    gain=gain_ref[...]
    for w in range(NW):
        sl=pl.ds(w*WT,WT)
        dx=dn_ref[sl,:].astype(bf16).astype(f32)*gain
        xh=xh_ref[sl,:]
        d=rstd_ref[sl,:]*(dx-jnp.mean(dx,-1,keepdims=True)-xh*jnp.mean(dx*xh,-1,keepdims=True))
        dwin_ref[sl,:]=(back_ref[sl,:].astype(f32)+d).astype(bf16)

def tail_put(order_ref,dwin_ref,out_ref):
    row=order_ref[...]
    T=row.shape[1]
    for w in range(NW):
        sl=pl.ds(w*WT,WT)
        si=lax.broadcasted_iota(jnp.int32,(WT,T),0)+w*WT
        oh=jnp.where(si==row,1.0,0.0).astype(bf16)
        out_ref[sl,:]=dot(oh,dwin_ref[...]).astype(bf16)


def remote(src, dst, ss, rs, dev):
    return pltpu.make_async_remote_copy(
        src_ref=src, dst_ref=dst, send_sem=ss, recv_sem=rs, device_id=dev, device_id_type=MESH
    )


def split3(v):
    a = v.astype(bf16)
    r = v - a.astype(f32)
    b = r.astype(bf16)
    c = (r - b.astype(f32)).astype(bf16)
    return jnp.concatenate([a, b, c], 0)


def pieces(v):
    a = v.astype(bf16)
    r = v - a.astype(f32)
    b = r.astype(bf16)
    return a, b, (r - b.astype(f32)).astype(bf16)


def hdot(a, b):
    rows = a.shape[0]
    b1, b2, b3 = pieces(b)
    a3 = split3(a)
    u = dot(a3, b1)
    v = dot(a3[: 2 * rows], b2)
    w = dot(a3[:rows], b3)
    return u[:rows] + ((u[rows : 2 * rows] + v[:rows]) + (u[2 * rows :] + (v[rows:] + w)))


def inverse_factors(gram):
    lane = lax.broadcasted_iota(jnp.int32, (32, 128), 1)
    row = lax.broadcasted_iota(jnp.int32, (32, 128), 0)
    first = (lane % 64) < 32
    state = jnp.where(lane < 64, gram, jnp.where((lane % 32) == row, 1.0, 0.0))
    for j in range(31):
        cols = jnp.where(first, state[:, j : j + 1], state[:, 32 + j : 33 + j])
        factor = cols / cols[j : j + 1, :]
        state = state - jnp.where(row > j, factor, 0.0) * state[j : j + 1, :]
    out = []
    for k in range(2):
        diag = jnp.sum(jnp.where(lane == row + 32 * k, state, 0.0), axis=1, keepdims=True)
        out.append(state[:, 64 + 32 * k : 96 + 32 * k] * (1.0 / jnp.sqrt(diag)))
    return out


def kernel(
    scale,
    order_in, tok_in, cot_in, gain_in, w_in, wo_in, errq_in, erro_in, qq_in, qo_in,
    dtok_ref, R, left_ref, inv_ref, mq, mo,
    order_ref, tok_ref, cot_ref, gain_ref, w_ref, wo_ref, errq_ref, erro_ref, qq_ref, qo_ref, in_sem,
    W, WO, back, n, nt, xh, rstd, d, dn, qkvc,
    gbuf, xr, xm, zs, zr, gobuf, xro, xmo, zso, zro,
    lr, mb, mr, t1, ex, ez, S, bqi, boi,
    az_s, az_r, ax_s, ax_r, ay_s, ay_r, ac_s, ac_r,
    rx_s, rx_r, rz_s, rz_r, ro_s,
    l_s, l_r, e_s, e_r,
):
    r = lax.axis_index("rep")
    f = lax.axis_index("fsdp")
    y = r // 2
    c = r % 2
    z = f // 4
    x = f % 4

    def zp(dz):
        return (r, ((z + dz) % 8) * 4 + x)

    def xp(dx):
        return (r, z * 4 + (x + dx) % 4)

    def yp(dy):
        return (((y + dy) % 4) * 2 + c, f)

    cp = (y * 2 + 1 - c, f)

    def rp(k):
        return ((r + k) % 8, f)

    loads = [
        pltpu.make_async_copy(a, b, in_sem.at[k])
        for k, (a, b) in enumerate(
            (
                (w_in, w_ref), (wo_in, wo_ref), (order_in, order_ref), (gain_in, gain_ref), (tok_in, tok_ref),
                (cot_in, cot_ref), (errq_in, errq_ref), (erro_in, erro_ref), (qq_in, qq_ref), (qo_in, qo_ref),
            )
        )
    ]
    for cc in loads:
        cc.start()
    barrier = pltpu.get_barrier_semaphore()
    for k in range(1, 8):
        pl.semaphore_signal(barrier, inc=1, device_id=zp(k), device_id_type=MESH)
        pl.semaphore_signal(barrier, inc=1, device_id=rp(k), device_id_type=MESH)
    for k in range(1, 4):
        pl.semaphore_signal(barrier, inc=1, device_id=xp(k), device_id_type=MESH)

    def fr(w):
        front_window(w, order_ref, tok_ref, cot_ref, gain_ref, back, n, xh, rstd)

    source = (x // 2) == c
    for cc in loads[:2]:
        cc.wait()

    own = y % 2

    @pl.when(source)
    def _():
        for i in range(2):
            for k in range(3):
                W[2 * own + i, z, x, :, 128 * k : 128 * k + 128] = w_ref[
                    :, pl.ds(pl.multiple_of(512 * k + (2 * own + i) * 128, 128), 128)
                ]

        @pl.when((z // 4) == own)
        def _():
            WO[z, x] = wo_ref[...]

    pl.semaphore_wait(barrier, 17)

    def w_z(i, k, at):
        a = W.at[2 * own + i, at, x]
        return remote(a, a, az_s.at[i, k - 1], az_r.at[i, k - 1], zp(k))

    def wo_z(k, at):
        a = WO.at[at, x]
        return remote(a, a, az_s.at[2, k - 1], az_r.at[2, k - 1], zp(k))

    def w_x(i, k, at):
        a = W.at[2 * own + i, :, at]
        b = WO.at[pl.ds(2 * (2 * own + i), 2), at]
        return (
            remote(a, a, ax_s.at[0, i, k - 1], ax_r.at[0, i, k - 1], xp(k)),
            remote(b, b, ax_s.at[1, i, k - 1], ax_r.at[1, i, k - 1], xp(k)),
        )

    def wait_x(i):
        for k in range(1, 4):
            src = (x - k + 4) % 4

            @pl.when((src // 2) == c)
            def _():
                for cc in w_x(i, k, src):
                    cc.wait_recv()

    @pl.when(source)
    def _():
        for i in range(2):
            for k in range(1, 8):
                w_z(i, k, z).start()
            if i == 0:

                @pl.when((z // 4) == own)
                def _():
                    for k in range(1, 8):
                        wo_z(k, z).start()

    for cc in loads[2:6]:
        cc.wait()
    fr(0)
    fr(1)
    fr(2)

    @pl.when(source)
    def _():
        for i in range(2):
            for k in range(1, 8):
                src = (z - k + 8) % 8
                w_z(i, k, src).wait_recv()

                @pl.when((src // 2) == 2 * own + i)
                def _():
                    wo_z(k, src).wait_recv()

            for k in range(1, 4):
                for cc in w_x(i, k, x):
                    cc.start()

    fr(3)
    nt[...] = n[...].T

    def hp_of(s):
        return (2 * own + s) % 4

    def half(hp, core):
        return W.at[hp, :, pl.ds(2 * core, 2)], WO.at[pl.ds(2 * hp, 2), pl.ds(2 * core, 2)]

    def core_copy(s, core):
        a, b = half(hp_of(s), core)
        return (
            remote(a, a, ac_s.at[0, s], ac_r.at[0, s], cp),
            remote(b, b, ac_s.at[1, s], ac_r.at[1, s], cp),
        )

    def y_copy(i, hp):
        a, b = half(hp, c)
        to = yp((1 + 2 * own + 2 * i) % 4)
        return (
            remote(a, a, ay_s.at[0, i], ay_r.at[0, i], to),
            remote(b, b, ay_s.at[1, i], ay_r.at[1, i], to),
        )

    def spread(i):
        wait_x(i)
        for cc in y_copy(i, 2 * own + i):
            cc.start()
        for cc in core_copy(i, c):
            cc.start()

    spread(0)

    def x_copy(kind, s, way):
        to = xp(1 + 2 * way)
        h = 1 - way if kind == 1 else way
        if kind == 2:
            a, b = xm.at[s, way], xmo.at[s, pl.ds(way, 1)]
        else:
            at = (x + 2) % 4 if kind == 0 else (x + 1 + 2 * way) % 4
            a, b = gbuf.at[s, pl.ds(4 * h, 4), at], gobuf.at[s, pl.ds(h, 1), at]
        return (
            remote(a, xr.at[kind, s, way], rx_s.at[0, kind, s, way], rx_r.at[0, kind, s, way], to),
            remote(b, xro.at[kind, s, pl.ds(way, 1)], rx_s.at[1, kind, s, way], rx_r.at[1, kind, s, way], to),
        )

    def merge(s):
        for way in range(2):
            for cc in x_copy(0, s, way):
                cc.wait_recv()
            at = (x + 1 + 2 * way) % 4
            xm[s, way] = (gbuf[s, 4 * way : 4 * way + 4, at].astype(f32) + xr[0, s, way].astype(f32)).astype(bf16)
            xmo[s, way] = (gobuf[s, way, at].astype(f32) + xro[0, s, way].astype(f32)).astype(bf16)
            for cc in x_copy(2, s, way):
                cc.start()

    def z_send(s, k):
        return remote(
            zs.at[s, (z + k) % 8], zr.at[s, k - 1], rz_s.at[0, s, k - 1], rz_r.at[0, s, k - 1], zp(k)
        )

    def zo_send(s, j, k):
        return remote(zso.at[s, j], zro.at[k - 1], ro_s.at[s, j], rz_r.at[1, 0, k - 1], zp(k))

    def zo_each(s, act):
        for j in range(2):
            k = (2 * hp_of(s) + j - z + 8) % 8

            @pl.when(k > 0)
            def _():
                act(zo_send(s, j, k))

    def second(s):
        for kind in (1, 2):
            for way in range(2):
                for cc in x_copy(kind, s, way):
                    cc.wait_recv()
        for h in range(2):
            rows = slice(4 * h, 4 * h + 4)
            total = gbuf[s, rows, x].astype(f32) + (xr[1, s, 1 - h].astype(f32) + xr[2, s, h].astype(f32))
            zs[s, rows] = total.astype(bf16)
            total = gobuf[s, h, x].astype(f32) + (xro[1, s, 1 - h].astype(f32) + xro[2, s, h].astype(f32))
            zso[s, h] = total.astype(bf16)
        for k in range(1, 8):
            z_send(s, k).start()
        zo_each(s, lambda cc: cc.start())

    def step(s, carry):
        hp = hp_of(s)
        for cc in core_copy(s, 1 - c):
            cc.wait_recv()

        def mid():
            @pl.when(s == 0)
            def _():
                spread(1)

            @pl.when((s == 1) | (s == 2))
            def _():
                for cc in y_copy(s - 1, hp_of(s + 1)):
                    cc.wait_recv()
                for cc in core_copy(s + 1, c):
                    cc.start()

        def g_store(v):
            gbuf[s] = v.reshape(8, 4, 16, 384)

        def go_store(v):
            gobuf[s] = v.reshape(2, 4, 16, 512)

        pair(
            n, nt, back, W[hp].reshape(512, 384), WO[pl.ds(2 * hp, 2)].reshape(128, 512),
            d, dn, qkvc, scale, s == 0, g_store, go_store, mid,
        )
        for kind in (0, 1):
            for way in range(2):
                for cc in x_copy(kind, s, way):
                    cc.start()

        @pl.when(s > 0)
        def _():
            merge(s - 1)

        @pl.when(s > 1)
        def _():
            second(s - 2)

        return carry

    lax.fori_loop(0, 4, step, 0)

    merge(3)
    second(2)
    second(3)
    tail_norm(dn, xh, rstd, gain_ref, back, qkvc)
    tail_put(order_ref, qkvc, dtok_ref)

    for cc in loads[6:]:
        cc.wait()
    q = qq_ref[...].astype(f32).astype(bf16)
    zero = jnp.zeros((32, 1536), bf16)
    bqi[...] = jnp.concatenate([q, zero, q, zero], 0)
    q = qo_ref[...].astype(f32).astype(bf16)
    zero = jnp.zeros((32, 512), bf16)
    boi[...] = jnp.concatenate([zero, q, zero, q], 0)

    def collect(s, carry):
        hp = hp_of(s)
        total = zs[s, z].astype(f32)
        for k in range(1, 8):
            z_send(s, k).wait_recv()
            total = total + zr[s, k - 1].astype(f32)
        for k in range(3):
            at = pl.ds(pl.multiple_of(512 * k + hp * 128, 128), 128)
            mq[:, at] = total[:, 128 * k : 128 * k + 128] + errq_ref[:, at]
        return carry

    lax.fori_loop(0, 4, collect, 0)
    for k in range(1, 8):
        zo_send(0, 0, k).wait_recv()
    so = (z // 2 - 2 * own + 4) % 4
    total = zso[so, z % 2].astype(f32)
    for k in range(7):
        total = total + zro[k].astype(f32)
    mo[...] = total + erro_ref[...]

    mqv = mq[...]
    mov = mo[...]
    def m_copy(k):
        return remote(mb.at[(r + k) % 8], mr.at[k - 1], l_s.at[1, k - 1], l_r.at[1, k - 1], rp(k))

    def l_copy(k, at):
        return remote(lr.at[at], lr.at[at], l_s.at[0, k - 1], l_r.at[0, k - 1], rp(k))

    part = dnt(split3(mqv), bqi[...]) + dnt(split3(mov), boi[...])
    lr[r] = ((part[0:16] + part[16:32]) + part[32:48]) * (1.0 / 127.0)
    for k in range(1, 8):
        l_copy(k, r).start()
    for k in range(12):
        mb[k // 2, k % 2] = mqv[:, 128 * k : 128 * k + 128]
    for k in range(4):
        mb[6 + k // 2, k % 2] = mov[:, 128 * k : 128 * k + 128]
    for k in range(1, 8):
        m_copy(k).start()
    for k in range(1, 8):
        m_copy(k).wait_recv()
    total = mb[r]
    for k in range(7):
        total = total + mr[k]
    for k in range(1, 8):
        l_copy(k, (r - k + 8) % 8).wait_recv()
    left = lr[0]
    for k in range(1, 8):
        left = left + lr[k]
    left = left * 0.125
    left_ref[...] = left

    lt = left.T
    lane = lax.broadcasted_iota(jnp.int32, (16, 128), 1)
    full = hdot(lt, left)
    gram = jnp.where(
        lane < 64,
        jnp.where(lane < 32, full[0:16], full[32:48]),
        jnp.where(lane < 96, full[16:32], full[48:64]),
    )
    mine = jnp.where(r < 6, lt[0:32], lt[32:64])
    for j in range(2):
        t = hdot(mine, total[j])
        for k in range(2):
            t1[2 * j + k, 0:16] = t[16 * k : 16 * k + 16]
            t1[2 * j + k, 16:24] = gram[8 * k : 8 * k + 8]
    ex[x] = t1[x]

    def e_x(k, to, at):
        return remote(t1.at[to], ex.at[at], e_s.at[0, k - 1], e_r.at[0, k - 1], xp(k))

    def e_z(k, at):
        return remote(ez.at[at], ez.at[at], e_s.at[1, k - 1], e_r.at[1, k - 1], zp(k))

    def a_x(k, at):
        return remote(S.at[at], S.at[at], e_s.at[2, k - 1], e_r.at[2, k - 1], xp(k))

    def a_r(k, at):
        return remote(R.at[at], R.at[at], e_s.at[3, k - 1], e_r.at[3, k - 1], rp(k))

    for k in range(1, 4):
        e_x(k, (x + k) % 4, x).start()
    for k in range(1, 4):
        e_x(k, x, (x - k + 4) % 4).wait_recv()
    ez[z] = (ex[0] + ex[1]) + (ex[2] + ex[3])
    for k in range(1, 8):
        e_z(k, z).start()
    for k in range(1, 8):
        e_z(k, (z - k + 8) % 8).wait_recv()
    total = ez[0]
    for k in range(1, 8):
        total = total + ez[k]
    S[x] = total
    for k in range(1, 4):
        a_x(k, x).start()
    for k in range(1, 4):
        a_x(k, (x - k + 4) % 4).wait_recv()
    R[r] = S[:, 0:16]
    for k in range(1, 8):
        a_r(k, r).start()
    gram = jnp.concatenate([S[0, 16:24], S[1, 16:24]], 0)
    iq, io = inverse_factors(jnp.concatenate([gram, pltpu.roll(gram, 64, 1)], 0))
    inv_ref[0] = iq
    inv_ref[1] = io
    for k in range(1, 8):
        a_r(k, (r - k + 8) % 8).wait_recv()

    @pl.when(source)
    def _():
        for i in range(2):
            for k in range(1, 8):
                w_z(i, k, z).wait_send()
            for k in range(1, 4):
                for cc in w_x(i, k, x):
                    cc.wait_send()

        @pl.when((z // 4) == own)
        def _():
            for k in range(1, 8):
                wo_z(k, z).wait_send()

    for i in range(2):
        for cc in y_copy(i, 2 * own + i):
            cc.wait_send()

    def sent(s, carry):
        for cc in core_copy(s, c):
            cc.wait_send()
        for kind in range(3):
            for way in range(2):
                for cc in x_copy(kind, s, way):
                    cc.wait_send()
        for k in range(1, 8):
            z_send(s, k).wait_send()
        zo_each(s, lambda cc: cc.wait_send())
        return carry

    lax.fori_loop(0, 4, sent, 0)
    for k in range(1, 8):
        m_copy(k).wait_send()
        l_copy(k, r).wait_send()
        e_z(k, z).wait_send()
        a_r(k, r).wait_send()
    for k in range(1, 4):
        e_x(k, (x + k) % 4, x).wait_send()
        a_x(k, x).wait_send()


def finish(
    dtok_in, R, left_ref, inv_ref, mq_ref, mo_ref,
    dtok_out, gradq_out, grado_out, nerrq_out, nerro_out, bq_out, bo_out,
    gradq, grado, nerrq, nerro, bq, bo, sem,
):
    def out(k, a, b):
        cc = pltpu.make_async_copy(a, b, sem.at[k])
        cc.start()
        return cc

    outs = [out(0, dtok_in, dtok_out)]
    left = left_ref[...]
    iq = inv_ref[0]
    io = inv_ref[1]
    ortho_q = hdot(left[:, 0:32], iq.T)
    ortho_o = hdot(left[:, 32:64], io.T)
    blocks = R[...].reshape(16, 32, 128)
    bq[...] = hdot(iq, jnp.concatenate([blocks[k] for k in range(12)], 1)) * 0.125
    outs.append(out(1, bq, bq_out))
    bo[...] = hdot(io, jnp.concatenate([blocks[12 + k] for k in range(4)], 1)) * 0.125
    outs.append(out(2, bo, bo_out))
    grad = hdot(ortho_q, bq[...])
    gradq[...] = grad
    nerrq[...] = mq_ref[...] - grad
    outs.append(out(3, gradq, gradq_out))
    outs.append(out(4, nerrq, nerrq_out))
    grad = hdot(ortho_o, bo[...])
    grado[...] = grad
    nerro[...] = mo_ref[...] - grad
    outs.append(out(5, grado, grado_out))
    outs.append(out(6, nerro, nerro_out))
    for cc in outs:
        cc.wait()


def per_device(tokens, cotangent, window_order, gain, w_qkv, w_out, err_qkv, err_out, q_qkv, q_out):
    scale = float(lax.axis_size("fsdp") * tokens.shape[0]) ** (-0.5)
    vmem = pl.BlockSpec(memory_space=pltpu.VMEM)
    V = pltpu.VMEM
    dma = pltpu.SemaphoreType.DMA
    hbm = pl.BlockSpec(memory_space=pl.ANY)

    def shape(dims, kind=f32):
        return jax.ShapeDtypeStruct(dims, kind)

    mid = pl.pallas_call(
        functools.partial(kernel, scale),
        out_shape=(
            shape((576, 512), bf16), shape((8, 4, 16, 128)), shape((16, 128)), shape((2, 32, 32)),
            shape((16, 1536)), shape((16, 512)),
        ),
        in_specs=[hbm] * 10,
        out_specs=(vmem,) * 6,
        scratch_shapes=[
            V((1, 576), jnp.int32), V((576, 512), bf16), V((576, 512), bf16), V((1, 512), f32),
            V((16, 1536), bf16), V((16, 512), bf16), V((16, 1536), f32), V((16, 512), f32),
            V((32, 1536), jnp.int32), V((32, 512), jnp.int32), dma((10,)),
            V((4, 8, 4, 16, 384), bf16), V((8, 4, 16, 512), bf16),
            V((576, 512), bf16), V((576, 512), bf16), V((512, 576), bf16),
            V((576, 512), f32), V((576, 1), f32), V((576, 384), bf16), V((576, 512), f32), V((576, 512), bf16),
            V((4, 8, 4, 16, 384), bf16), V((3, 4, 2, 4, 16, 384), bf16), V((4, 2, 4, 16, 384), bf16), V((4, 8, 16, 384), bf16), V((4, 7, 16, 384), bf16),
            V((4, 2, 4, 16, 512), bf16), V((3, 4, 2, 16, 512), bf16), V((4, 2, 16, 512), bf16), V((4, 2, 16, 512), bf16), V((7, 16, 512), bf16),
            V((8, 16, 128), f32), V((8, 2, 16, 128), f32), V((7, 2, 16, 128), f32),
            V((4, 24, 128), f32), V((4, 24, 128), f32), V((8, 24, 128), f32), V((4, 24, 128), f32),
            V((128, 1536), bf16), V((128, 512), bf16),
            dma((3, 7)), dma((3, 7)), dma((2, 2, 3)), dma((2, 2, 3)), dma((2, 2)), dma((2, 2)), dma((2, 4)), dma((2, 4)),
            dma((2, 3, 4, 2)), dma((2, 3, 4, 2)), dma((1, 4, 7)), dma((2, 4, 7)), dma((4, 2)),
            dma((2, 7)), dma((2, 7)), dma((4, 7)), dma((4, 7)),
        ],
        compiler_params=pltpu.CompilerParams(
            collective_id=0, has_side_effects=True, vmem_limit_bytes=56 * 2**20
        ),
    )(
        window_order, tokens, cotangent, gain.reshape(1, 512), w_qkv, w_out,
        err_qkv.reshape(16, 1536), err_out.reshape(16, 512), q_qkv.T, q_out.T,
    )
    dt, gq, go, eq, eo, bq, bo = pl.pallas_call(
        finish,
        out_shape=(
            shape((576, 512), bf16), shape((16, 1536)), shape((16, 512)), shape((16, 1536)), shape((16, 512)),
            shape((32, 1536)), shape((32, 512)),
        ),
        in_specs=[vmem] * 6,
        out_specs=(hbm,) * 7,
        scratch_shapes=[
            V((16, 1536), f32), V((16, 512), f32), V((16, 1536), f32), V((16, 512), f32),
            V((32, 1536), f32), V((32, 512), f32), dma((7,)),
        ],
    )(*mid)
    return dt, gq, go, eq[None], eo[None], bq.T, bo.T


def solution(mesh):
    return jax.shard_map(
        per_device,
        mesh=mesh,
        in_specs=(
            P(("rep", "fsdp"), None),
            P(("rep", "fsdp"), None),
            P(("rep", "fsdp"), None),
            P(),
            P("fsdp", None),
            P("fsdp", None),
            P("rep", "fsdp", None),
            P("rep", "fsdp", None),
            P(),
            P(),
        ),
        out_specs=(
            P(("rep", "fsdp"), None),
            P("fsdp", None),
            P("fsdp", None),
            P("rep", "fsdp", None),
            P("rep", "fsdp", None),
            P(),
            P(),
        ),
        check_vma=False,
    )
```

```python
import functools

import jax
import jax.numpy as jnp
from jax import lax
from jax.experimental import pallas as pl
from jax.experimental.pallas import tpu as pltpu
from jax.sharding import PartitionSpec as P

f32 = jnp.float32
bf16 = jnp.bfloat16
MESH = pl.DeviceIdType.MESH
def dot(a,b): return jnp.dot(a,b,preferred_element_type=f32)
def dnt(a,b): return lax.dot_general(a,b,(((1,),(1,)),((),())),preferred_element_type=f32)
WT=144; NW=4
LOG2E=1.4426950408889634
def front_window(w,order_ref,tok_ref,cot_ref,gain_ref,back_ref,n_ref,xh_ref,rstd_ref):
        row=order_ref[...]
        T=row.shape[1]
        gain=gain_ref[...]
        sl=pl.ds(w*WT,WT)
        si=lax.broadcasted_iota(jnp.int32,(WT,T),0)+w*WT
        li=lax.broadcasted_iota(jnp.int32,(WT,T),1)
        col=jnp.sum(jnp.where(si==li,row,0).astype(f32),axis=1,keepdims=True).astype(jnp.int32)
        oh=jnp.where(col==li,1.0,0.0).astype(bf16)
        x=dot(oh,tok_ref[...])
        back_ref[sl,:]=dot(oh,cot_ref[...]).astype(bf16)
        ce=x-jnp.mean(x,-1,keepdims=True)
        rs=lax.rsqrt(jnp.mean(ce*ce,-1,keepdims=True)+1e-5)
        xh=ce*rs
        xh_ref[sl,:]=xh
        rstd_ref[sl,:]=rs
        n=(xh*gain).astype(bf16)
        n_ref[sl,:]=n
def pair(n_ref,nt_ref,back_ref,W,WO,d_ref,dn_ref,qkvc_ref,scale,first,g_store,go_store,mid=None):
    qkvc_ref[:,:384]=dot(n_ref[...],W).astype(bf16)
    qkvc_ref[:,384:]=dnt(back_ref[...],WO).astype(bf16)
    if mid is not None: mid()
    lane=lax.broadcasted_iota(jnp.int32,(WT,128),1)
    go=jnp.zeros((128,512),f32)
    z=jnp.zeros((),bf16)
    lo=lane<64
    def two(a): return jnp.concatenate([jnp.where(lo,a,z),jnp.where(lo,z,a)],0)
    for w0 in range(0,NW,4):
        ws=range(w0,w0+4)
        sd={}
        for w in ws:
            sl=pl.ds(w*WT,WT)
            q=qkvc_ref[sl,0:128]; k=qkvc_ref[sl,128:256]; v=qkvc_ref[sl,256:384]; c=qkvc_ref[sl,384:512]
            sd[w]=(dnt(two(k),q),dnt(two(v),c))
        pd={}
        for w in ws:
            s2,d2=sd[w]
            ps=[];dss=[]
            for h in range(2):
                s=s2[WT*h:WT*h+WT]
                mx=jnp.max(s,axis=0,keepdims=True)
                e=jnp.exp2((s-mx)*(0.125*LOG2E))
                wt=e*(1.0/jnp.sum(e,axis=0,keepdims=True))
                p=wt.astype(bf16)
                dp=d2[WT*h:WT*h+WT].astype(bf16).astype(f32)
                t=wt*dp
                ds=(t-wt*jnp.sum(t,axis=0,keepdims=True)).astype(bf16)
                ps.append(p);dss.append(ds)
            pd[w]=(ps,dss)
        for w in ws:
            sl=pl.ds(w*WT,WT)
            ps,dss=pd[w]
            q=qkvc_ref[sl,0:128]; k=qkvc_ref[sl,128:256]; v=qkvc_ref[sl,256:384]; c=qkvc_ref[sl,384:512]
            kt=k.T; vt=v.T
            cts=[dot(vt[:64],ps[0]),dot(vt[64:],ps[1])]
            dqs=[dot(kt[:64],dss[0]),dot(kt[64:],dss[1])]
            dv=jnp.where(lo,dot(ps[0],c),dot(ps[1],c))
            dk=jnp.where(lo,dot(dss[0],q),dot(dss[1],q))
            ctx=jnp.concatenate(cts,0).astype(bf16)
            go=go+dot(ctx,back_ref[sl,:])
            dq=(jnp.concatenate(dqs,0)*0.125).astype(bf16).T
            d_ref[sl,0:128]=dq
            d_ref[sl,128:256]=(dk*0.125).astype(bf16)
            d_ref[sl,256:384]=dv.astype(bf16)
    go_store((go*scale).astype(bf16))
    g_store((dot(nt_ref[...],d_ref[...])*scale).astype(bf16))
    dn=dnt(d_ref[...],W)
    dn_ref[...]=jnp.where(first,0.0,dn_ref[...])+dn
def tail_norm(dn_ref,xh_ref,rstd_ref,gain_ref,back_ref,dwin_ref):
    gain=gain_ref[...]
    for w in range(NW):
        sl=pl.ds(w*WT,WT)
        dx=dn_ref[sl,:].astype(bf16).astype(f32)*gain
        xh=xh_ref[sl,:]
        d=rstd_ref[sl,:]*(dx-jnp.mean(dx,-1,keepdims=True)-xh*jnp.mean(dx*xh,-1,keepdims=True))
        dwin_ref[sl,:]=(back_ref[sl,:].astype(f32)+d).astype(bf16)

def tail_put(order_ref,dwin_ref,out_ref):
    row=order_ref[...]
    T=row.shape[1]
    for w in range(NW):
        sl=pl.ds(w*WT,WT)
        si=lax.broadcasted_iota(jnp.int32,(WT,T),0)+w*WT
        oh=jnp.where(si==row,1.0,0.0).astype(bf16)
        out_ref[sl,:]=dot(oh,dwin_ref[...]).astype(bf16)


def remote(src, dst, ss, rs, dev):
    return pltpu.make_async_remote_copy(
        src_ref=src, dst_ref=dst, send_sem=ss, recv_sem=rs, device_id=dev, device_id_type=MESH
    )


def split3(v):
    a = v.astype(bf16)
    r = v - a.astype(f32)
    b = r.astype(bf16)
    c = (r - b.astype(f32)).astype(bf16)
    return jnp.concatenate([a, b, c], 0)


def pieces(v):
    a = v.astype(bf16)
    r = v - a.astype(f32)
    b = r.astype(bf16)
    return a, b, (r - b.astype(f32)).astype(bf16)


def hdot(a, b):
    rows = a.shape[0]
    b1, b2, b3 = pieces(b)
    a3 = split3(a)
    u = dot(a3, b1)
    v = dot(a3[: 2 * rows], b2)
    w = dot(a3[:rows], b3)
    return u[:rows] + ((u[rows : 2 * rows] + v[:rows]) + (u[2 * rows :] + (v[rows:] + w)))


def inverse_factors(gram):
    lane = lax.broadcasted_iota(jnp.int32, (32, 128), 1)
    row = lax.broadcasted_iota(jnp.int32, (32, 128), 0)
    first = (lane % 64) < 32
    state = jnp.where(lane < 64, gram, jnp.where((lane % 32) == row, 1.0, 0.0))
    for j in range(31):
        cols = jnp.where(first, state[:, j : j + 1], state[:, 32 + j : 33 + j])
        factor = cols / cols[j : j + 1, :]
        state = state - jnp.where(row > j, factor, 0.0) * state[j : j + 1, :]
    out = []
    for k in range(2):
        diag = jnp.sum(jnp.where(lane == row + 32 * k, state, 0.0), axis=1, keepdims=True)
        out.append(state[:, 64 + 32 * k : 96 + 32 * k] * (1.0 / jnp.sqrt(diag)))
    return out


def kernel(
    scale,
    order_in, tok_in, cot_in, gain_in, w_in, wo_in, errq_in, erro_in, qq_in, qo_in,
    dtok_ref, R, left_ref, inv_ref, mq, mo,
    order_ref, tok_ref, cot_ref, gain_ref, w_ref, wo_ref, errq_ref, erro_ref, qq_ref, qo_ref, in_sem,
    W, WO, back, n, nt, xh, rstd, d, dn, qkvc,
    gbuf, xr, xm, zs, zr, gobuf, xro, xmo, zso, zro,
    lr, mb, mr, t1, ex, ez, S, bqi, boi,
    az_s, az_r, ax_s, ax_r, ay_s, ay_r, ac_s, ac_r,
    rx_s, rx_r, rz_s, rz_r, ro_s,
    l_s, l_r, e_s, e_r,
):
    r = lax.axis_index("rep")
    f = lax.axis_index("fsdp")
    y = r // 2
    c = r % 2
    z = f // 4
    x = f % 4

    def zp(dz):
        return (r, ((z + dz) % 8) * 4 + x)

    def xp(dx):
        return (r, z * 4 + (x + dx) % 4)

    def yp(dy):
        return (((y + dy) % 4) * 2 + c, f)

    cp = (y * 2 + 1 - c, f)

    def rp(k):
        return ((r + k) % 8, f)

    loads = [
        pltpu.make_async_copy(a, b, in_sem.at[k])
        for k, (a, b) in enumerate(
            (
                (w_in, w_ref), (wo_in, wo_ref), (order_in, order_ref), (gain_in, gain_ref), (tok_in, tok_ref),
                (cot_in, cot_ref), (errq_in, errq_ref), (erro_in, erro_ref), (qq_in, qq_ref), (qo_in, qo_ref),
            )
        )
    ]
    for cc in loads:
        cc.start()
    barrier = pltpu.get_barrier_semaphore()
    for k in range(1, 8):
        pl.semaphore_signal(barrier, inc=1, device_id=zp(k), device_id_type=MESH)
        pl.semaphore_signal(barrier, inc=1, device_id=rp(k), device_id_type=MESH)
    for k in range(1, 4):
        pl.semaphore_signal(barrier, inc=1, device_id=xp(k), device_id_type=MESH)

    def fr(w):
        front_window(w, order_ref, tok_ref, cot_ref, gain_ref, back, n, xh, rstd)

    source = (x // 2) == c
    for cc in loads[:2]:
        cc.wait()

    own = y % 2

    @pl.when(source)
    def _():
        for i in range(2):
            for k in range(3):
                W[2 * own + i, z, x, :, 128 * k : 128 * k + 128] = w_ref[
                    :, pl.ds(pl.multiple_of(512 * k + (2 * own + i) * 128, 128), 128)
                ]

        @pl.when((z // 4) == own)
        def _():
            WO[z, x] = wo_ref[...]

    pl.semaphore_wait(barrier, 17)

    def w_z(i, k, at):
        a = W.at[2 * own + i, at, x]
        return remote(a, a, az_s.at[i, k - 1], az_r.at[i, k - 1], zp(k))

    def wo_z(k, at):
        a = WO.at[at, x]
        return remote(a, a, az_s.at[2, k - 1], az_r.at[2, k - 1], zp(k))

    def w_x(i, k, at):
        a = W.at[2 * own + i, :, at]
        b = WO.at[pl.ds(2 * (2 * own + i), 2), at]
        return (
            remote(a, a, ax_s.at[0, i, k - 1], ax_r.at[0, i, k - 1], xp(k)),
            remote(b, b, ax_s.at[1, i, k - 1], ax_r.at[1, i, k - 1], xp(k)),
        )

    def wait_x(i):
        for k in range(1, 4):
            src = (x - k + 4) % 4

            @pl.when((src // 2) == c)
            def _():
                for cc in w_x(i, k, src):
                    cc.wait_recv()

    @pl.when(source)
    def _():
        for i in range(2):
            for k in range(1, 8):
                w_z(i, k, z).start()
            if i == 0:

                @pl.when((z // 4) == own)
                def _():
                    for k in range(1, 8):
                        wo_z(k, z).start()

    for cc in loads[2:6]:
        cc.wait()
    fr(0)
    fr(1)
    fr(2)

    @pl.when(source)
    def _():
        for i in range(2):
            for k in range(1, 8):
                src = (z - k + 8) % 8
                w_z(i, k, src).wait_recv()

                @pl.when((src // 2) == 2 * own + i)
                def _():
                    wo_z(k, src).wait_recv()

            for k in range(1, 4):
                for cc in w_x(i, k, x):
                    cc.start()

    fr(3)
    nt[...] = n[...].T

    def hp_of(s):
        return (2 * own + s) % 4

    def half(hp, core):
        return W.at[hp, :, pl.ds(2 * core, 2)], WO.at[pl.ds(2 * hp, 2), pl.ds(2 * core, 2)]

    def core_copy(s, core):
        a, b = half(hp_of(s), core)
        return (
            remote(a, a, ac_s.at[0, s], ac_r.at[0, s], cp),
            remote(b, b, ac_s.at[1, s], ac_r.at[1, s], cp),
        )

    def y_copy(i, hp):
        out = []
        for way in range(2):
            a = W.at[hp, pl.ds(4 * way, 4), pl.ds(2 * c, 2)]
            b = WO.at[pl.ds(2 * hp + way, 1), pl.ds(2 * c, 2)]
            to = yp(1 + 2 * way)
            out.append(remote(a, a, ay_s.at[0, i, way], ay_r.at[0, i, way], to))
            out.append(remote(b, b, ay_s.at[1, i, way], ay_r.at[1, i, way], to))
        return out

    def spread(i):
        wait_x(i)
        for cc in y_copy(i, 2 * own + i):
            cc.start()
        for cc in core_copy(i, c):
            cc.start()

    spread(0)

    def x_copy(kind, s, way):
        to = xp(1 + 2 * way)
        h = 1 - way if kind == 1 else way
        if kind == 2:
            a, b = xm.at[s, way], xmo.at[s, pl.ds(way, 1)]
        else:
            at = (x + 2) % 4 if kind == 0 else (x + 1 + 2 * way) % 4
            a, b = gbuf.at[s, pl.ds(4 * h, 4), at], gobuf.at[s, pl.ds(h, 1), at]
        return (
            remote(a, xr.at[kind, s, way], rx_s.at[0, kind, s, way], rx_r.at[0, kind, s, way], to),
            remote(b, xro.at[kind, s, pl.ds(way, 1)], rx_s.at[1, kind, s, way], rx_r.at[1, kind, s, way], to),
        )

    def merge(s):
        for way in range(2):
            for cc in x_copy(0, s, way):
                cc.wait_recv()
            at = (x + 1 + 2 * way) % 4
            xm[s, way] = (gbuf[s, 4 * way : 4 * way + 4, at].astype(f32) + xr[0, s, way].astype(f32)).astype(bf16)
            xmo[s, way] = (gobuf[s, way, at].astype(f32) + xro[0, s, way].astype(f32)).astype(bf16)
            for cc in x_copy(2, s, way):
                cc.start()

    def z_send(s, k):
        return remote(
            zs.at[s, (z + k) % 8], zr.at[s, k - 1], rz_s.at[0, s, k - 1], rz_r.at[0, s, k - 1], zp(k)
        )

    def zo_send(s, j, k):
        return remote(zso.at[s, j], zro.at[k - 1], ro_s.at[s, j], rz_r.at[1, 0, k - 1], zp(k))

    def zo_each(s, act):
        for j in range(2):
            k = (2 * hp_of(s) + j - z + 8) % 8

            @pl.when(k > 0)
            def _():
                act(zo_send(s, j, k))

    def second(s):
        for kind in (1, 2):
            for way in range(2):
                for cc in x_copy(kind, s, way):
                    cc.wait_recv()
        for h in range(2):
            rows = slice(4 * h, 4 * h + 4)
            total = gbuf[s, rows, x].astype(f32) + (xr[1, s, 1 - h].astype(f32) + xr[2, s, h].astype(f32))
            zs[s, rows] = total.astype(bf16)
            total = gobuf[s, h, x].astype(f32) + (xro[1, s, 1 - h].astype(f32) + xro[2, s, h].astype(f32))
            zso[s, h] = total.astype(bf16)
        for k in range(1, 8):
            z_send(s, k).start()
        zo_each(s, lambda cc: cc.start())

    def step(s, carry):
        hp = hp_of(s)
        for cc in core_copy(s, 1 - c):
            cc.wait_recv()

        def mid():
            @pl.when(s == 0)
            def _():
                spread(1)

            @pl.when((s == 1) | (s == 2))
            def _():
                for cc in y_copy(s - 1, hp_of(s + 1)):
                    cc.wait_recv()
                for cc in core_copy(s + 1, c):
                    cc.start()

        def g_store(v):
            gbuf[s] = v.reshape(8, 4, 16, 384)

        def go_store(v):
            gobuf[s] = v.reshape(2, 4, 16, 512)

        pair(
            n, nt, back, W[hp].reshape(512, 384), WO[pl.ds(2 * hp, 2)].reshape(128, 512),
            d, dn, qkvc, scale, s == 0, g_store, go_store, mid,
        )
        for kind in (0, 1):
            for way in range(2):
                for cc in x_copy(kind, s, way):
                    cc.start()

        @pl.when(s > 0)
        def _():
            merge(s - 1)

        @pl.when(s > 1)
        def _():
            second(s - 2)

        return carry

    lax.fori_loop(0, 4, step, 0)

    merge(3)
    second(2)
    second(3)
    tail_norm(dn, xh, rstd, gain_ref, back, qkvc)
    tail_put(order_ref, qkvc, dtok_ref)

    for cc in loads[6:]:
        cc.wait()
    q = qq_ref[...].astype(f32).astype(bf16)
    zero = jnp.zeros((32, 1536), bf16)
    bqi[...] = jnp.concatenate([q, zero, q, zero], 0)
    q = qo_ref[...].astype(f32).astype(bf16)
    zero = jnp.zeros((32, 512), bf16)
    boi[...] = jnp.concatenate([zero, q, zero, q], 0)

    def collect(s, carry):
        hp = hp_of(s)
        total = zs[s, z].astype(f32)
        for k in range(1, 8):
            z_send(s, k).wait_recv()
            total = total + zr[s, k - 1].astype(f32)
        for k in range(3):
            at = pl.ds(pl.multiple_of(512 * k + hp * 128, 128), 128)
            mq[:, at] = total[:, 128 * k : 128 * k + 128] + errq_ref[:, at]
        return carry

    lax.fori_loop(0, 4, collect, 0)
    for k in range(1, 8):
        zo_send(0, 0, k).wait_recv()
    so = (z // 2 - 2 * own + 4) % 4
    total = zso[so, z % 2].astype(f32)
    for k in range(7):
        total = total + zro[k].astype(f32)
    mo[...] = total + erro_ref[...]

    mqv = mq[...]
    mov = mo[...]
    def m_copy(k):
        return remote(mb.at[(r + k) % 8], mr.at[k - 1], l_s.at[1, k - 1], l_r.at[1, k - 1], rp(k))

    def l_copy(k, at):
        return remote(lr.at[at], lr.at[at], l_s.at[0, k - 1], l_r.at[0, k - 1], rp(k))

    part = dnt(split3(mqv), bqi[...]) + dnt(split3(mov), boi[...])
    lr[r] = ((part[0:16] + part[16:32]) + part[32:48]) * (1.0 / 127.0)
    for k in range(1, 8):
        l_copy(k, r).start()
    for k in range(12):
        mb[k // 2, k % 2] = mqv[:, 128 * k : 128 * k + 128]
    for k in range(4):
        mb[6 + k // 2, k % 2] = mov[:, 128 * k : 128 * k + 128]
    for k in range(1, 8):
        m_copy(k).start()
    for k in range(1, 8):
        m_copy(k).wait_recv()
    total = mb[r]
    for k in range(7):
        total = total + mr[k]
    for k in range(1, 8):
        l_copy(k, (r - k + 8) % 8).wait_recv()
    left = lr[0]
    for k in range(1, 8):
        left = left + lr[k]
    left = left * 0.125
    left_ref[...] = left

    lt = left.T
    lane = lax.broadcasted_iota(jnp.int32, (16, 128), 1)
    full = hdot(lt, left)
    gram = jnp.where(
        lane < 64,
        jnp.where(lane < 32, full[0:16], full[32:48]),
        jnp.where(lane < 96, full[16:32], full[48:64]),
    )
    mine = jnp.where(r < 6, lt[0:32], lt[32:64])
    for j in range(2):
        t = hdot(mine, total[j])
        for k in range(2):
            t1[2 * j + k, 0:16] = t[16 * k : 16 * k + 16]
            t1[2 * j + k, 16:24] = gram[8 * k : 8 * k + 8]
    ex[x] = t1[x]

    def e_x(k, to, at):
        return remote(t1.at[to], ex.at[at], e_s.at[0, k - 1], e_r.at[0, k - 1], xp(k))

    def e_z(k, at):
        return remote(ez.at[at], ez.at[at], e_s.at[1, k - 1], e_r.at[1, k - 1], zp(k))

    def a_x(k, at):
        return remote(S.at[at], S.at[at], e_s.at[2, k - 1], e_r.at[2, k - 1], xp(k))

    def a_r(k, at):
        return remote(R.at[at], R.at[at], e_s.at[3, k - 1], e_r.at[3, k - 1], rp(k))

    for k in range(1, 4):
        e_x(k, (x + k) % 4, x).start()
    for k in range(1, 4):
        e_x(k, x, (x - k + 4) % 4).wait_recv()
    ez[z] = (ex[0] + ex[1]) + (ex[2] + ex[3])
    for k in range(1, 8):
        e_z(k, z).start()
    for k in range(1, 8):
        e_z(k, (z - k + 8) % 8).wait_recv()
    total = ez[0]
    for k in range(1, 8):
        total = total + ez[k]
    S[x] = total
    for k in range(1, 4):
        a_x(k, x).start()
    for k in range(1, 4):
        a_x(k, (x - k + 4) % 4).wait_recv()
    R[r] = S[:, 0:16]
    for k in range(1, 8):
        a_r(k, r).start()
    gram = jnp.concatenate([S[0, 16:24], S[1, 16:24]], 0)
    iq, io = inverse_factors(jnp.concatenate([gram, pltpu.roll(gram, 64, 1)], 0))
    inv_ref[0] = iq
    inv_ref[1] = io
    for k in range(1, 8):
        a_r(k, (r - k + 8) % 8).wait_recv()

    @pl.when(source)
    def _():
        for i in range(2):
            for k in range(1, 8):
                w_z(i, k, z).wait_send()
            for k in range(1, 4):
                for cc in w_x(i, k, x):
                    cc.wait_send()

        @pl.when((z // 4) == own)
        def _():
            for k in range(1, 8):
                wo_z(k, z).wait_send()

    for i in range(2):
        for cc in y_copy(i, 2 * own + i):
            cc.wait_send()

    def sent(s, carry):
        for cc in core_copy(s, c):
            cc.wait_send()
        for kind in range(3):
            for way in range(2):
                for cc in x_copy(kind, s, way):
                    cc.wait_send()
        for k in range(1, 8):
            z_send(s, k).wait_send()
        zo_each(s, lambda cc: cc.wait_send())
        return carry

    lax.fori_loop(0, 4, sent, 0)
    for k in range(1, 8):
        m_copy(k).wait_send()
        l_copy(k, r).wait_send()
        e_z(k, z).wait_send()
        a_r(k, r).wait_send()
    for k in range(1, 4):
        e_x(k, (x + k) % 4, x).wait_send()
        a_x(k, x).wait_send()


def finish(
    dtok_in, R, left_ref, inv_ref, mq_ref, mo_ref,
    dtok_out, gradq_out, grado_out, nerrq_out, nerro_out, bq_out, bo_out,
    gradq, grado, nerrq, nerro, bq, bo, sem,
):
    def out(k, a, b):
        cc = pltpu.make_async_copy(a, b, sem.at[k])
        cc.start()
        return cc

    outs = [out(0, dtok_in, dtok_out)]
    left = left_ref[...]
    iq = inv_ref[0]
    io = inv_ref[1]
    ortho_q = hdot(left[:, 0:32], iq.T)
    ortho_o = hdot(left[:, 32:64], io.T)
    blocks = R[...].reshape(16, 32, 128)
    bq[...] = hdot(iq, jnp.concatenate([blocks[k] for k in range(12)], 1)) * 0.125
    outs.append(out(1, bq, bq_out))
    bo[...] = hdot(io, jnp.concatenate([blocks[12 + k] for k in range(4)], 1)) * 0.125
    outs.append(out(2, bo, bo_out))
    grad = hdot(ortho_q, bq[...])
    gradq[...] = grad
    nerrq[...] = mq_ref[...] - grad
    outs.append(out(3, gradq, gradq_out))
    outs.append(out(4, nerrq, nerrq_out))
    grad = hdot(ortho_o, bo[...])
    grado[...] = grad
    nerro[...] = mo_ref[...] - grad
    outs.append(out(5, grado, grado_out))
    outs.append(out(6, nerro, nerro_out))
    for cc in outs:
        cc.wait()


def per_device(tokens, cotangent, window_order, gain, w_qkv, w_out, err_qkv, err_out, q_qkv, q_out):
    scale = float(lax.axis_size("fsdp") * tokens.shape[0]) ** (-0.5)
    vmem = pl.BlockSpec(memory_space=pltpu.VMEM)
    V = pltpu.VMEM
    dma = pltpu.SemaphoreType.DMA
    hbm = pl.BlockSpec(memory_space=pl.ANY)

    def shape(dims, kind=f32):
        return jax.ShapeDtypeStruct(dims, kind)

    mid = pl.pallas_call(
        functools.partial(kernel, scale),
        out_shape=(
            shape((576, 512), bf16), shape((8, 4, 16, 128)), shape((16, 128)), shape((2, 32, 32)),
            shape((16, 1536)), shape((16, 512)),
        ),
        in_specs=[hbm] * 10,
        out_specs=(vmem,) * 6,
        scratch_shapes=[
            V((1, 576), jnp.int32), V((576, 512), bf16), V((576, 512), bf16), V((1, 512), f32),
            V((16, 1536), bf16), V((16, 512), bf16), V((16, 1536), f32), V((16, 512), f32),
            V((32, 1536), jnp.int32), V((32, 512), jnp.int32), dma((10,)),
            V((4, 8, 4, 16, 384), bf16), V((8, 4, 16, 512), bf16),
            V((576, 512), bf16), V((576, 512), bf16), V((512, 576), bf16),
            V((576, 512), f32), V((576, 1), f32), V((576, 384), bf16), V((576, 512), f32), V((576, 512), bf16),
            V((4, 8, 4, 16, 384), bf16), V((3, 4, 2, 4, 16, 384), bf16), V((4, 2, 4, 16, 384), bf16), V((4, 8, 16, 384), bf16), V((4, 7, 16, 384), bf16),
            V((4, 2, 4, 16, 512), bf16), V((3, 4, 2, 16, 512), bf16), V((4, 2, 16, 512), bf16), V((4, 2, 16, 512), bf16), V((7, 16, 512), bf16),
            V((8, 16, 128), f32), V((8, 2, 16, 128), f32), V((7, 2, 16, 128), f32),
            V((4, 24, 128), f32), V((4, 24, 128), f32), V((8, 24, 128), f32), V((4, 24, 128), f32),
            V((128, 1536), bf16), V((128, 512), bf16),
            dma((3, 7)), dma((3, 7)), dma((2, 2, 3)), dma((2, 2, 3)), dma((2, 2, 2)), dma((2, 2, 2)), dma((2, 4)), dma((2, 4)),
            dma((2, 3, 4, 2)), dma((2, 3, 4, 2)), dma((1, 4, 7)), dma((2, 4, 7)), dma((4, 2)),
            dma((2, 7)), dma((2, 7)), dma((4, 7)), dma((4, 7)),
        ],
        compiler_params=pltpu.CompilerParams(
            collective_id=0, has_side_effects=True, vmem_limit_bytes=56 * 2**20
        ),
    )(
        window_order, tokens, cotangent, gain.reshape(1, 512), w_qkv, w_out,
        err_qkv.reshape(16, 1536), err_out.reshape(16, 512), q_qkv.T, q_out.T,
    )
    dt, gq, go, eq, eo, bq, bo = pl.pallas_call(
        finish,
        out_shape=(
            shape((576, 512), bf16), shape((16, 1536)), shape((16, 512)), shape((16, 1536)), shape((16, 512)),
            shape((32, 1536)), shape((32, 512)),
        ),
        in_specs=[vmem] * 6,
        out_specs=(hbm,) * 7,
        scratch_shapes=[
            V((16, 1536), f32), V((16, 512), f32), V((16, 1536), f32), V((16, 512), f32),
            V((32, 1536), f32), V((32, 512), f32), dma((7,)),
        ],
    )(*mid)
    return dt, gq, go, eq[None], eo[None], bq.T, bo.T


def solution(mesh):
    return jax.shard_map(
        per_device,
        mesh=mesh,
        in_specs=(
            P(("rep", "fsdp"), None),
            P(("rep", "fsdp"), None),
            P(("rep", "fsdp"), None),
            P(),
            P("fsdp", None),
            P("fsdp", None),
            P("rep", "fsdp", None),
            P("rep", "fsdp", None),
            P(),
            P(),
        ),
        out_specs=(
            P(("rep", "fsdp"), None),
            P("fsdp", None),
            P("fsdp", None),
            P("rep", "fsdp", None),
            P("rep", "fsdp", None),
            P(),
            P(),
        ),
        check_vma=False,
    )
```

```python
import functools

import jax
import jax.numpy as jnp
from jax import lax
from jax.experimental import pallas as pl
from jax.experimental.pallas import tpu as pltpu
from jax.sharding import PartitionSpec as P

f32 = jnp.float32
bf16 = jnp.bfloat16
MESH = pl.DeviceIdType.MESH
FAR = (4, 3, 5, 2, 6, 1, 7)
def dot(a,b): return jnp.dot(a,b,preferred_element_type=f32)
def dnt(a,b): return lax.dot_general(a,b,(((1,),(1,)),((),())),preferred_element_type=f32)
WT=144; NW=4
LOG2E=1.4426950408889634
def front_window(w,order_ref,tok_ref,cot_ref,gain_ref,back_ref,n_ref,xh_ref,rstd_ref):
        row=order_ref[...]
        T=row.shape[1]
        gain=gain_ref[...]
        sl=pl.ds(w*WT,WT)
        si=lax.broadcasted_iota(jnp.int32,(WT,T),0)+w*WT
        li=lax.broadcasted_iota(jnp.int32,(WT,T),1)
        col=jnp.sum(jnp.where(si==li,row,0).astype(f32),axis=1,keepdims=True).astype(jnp.int32)
        oh=jnp.where(col==li,1.0,0.0).astype(bf16)
        x=dot(oh,tok_ref[...])
        back_ref[sl,:]=dot(oh,cot_ref[...]).astype(bf16)
        ce=x-jnp.mean(x,-1,keepdims=True)
        rs=lax.rsqrt(jnp.mean(ce*ce,-1,keepdims=True)+1e-5)
        xh=ce*rs
        xh_ref[sl,:]=xh
        rstd_ref[sl,:]=rs
        n=(xh*gain).astype(bf16)
        n_ref[sl,:]=n
def pair(n_ref,nt_ref,back_ref,W,WO,d_ref,dn_ref,qkvc_ref,scale,first,g_store,go_store,mid=None):
    qkvc_ref[:,:384]=dot(n_ref[...],W).astype(bf16)
    qkvc_ref[:,384:]=dnt(back_ref[...],WO).astype(bf16)
    if mid is not None: mid()
    lane=lax.broadcasted_iota(jnp.int32,(WT,128),1)
    go=jnp.zeros((128,512),f32)
    z=jnp.zeros((),bf16)
    lo=lane<64
    def two(a): return jnp.concatenate([jnp.where(lo,a,z),jnp.where(lo,z,a)],0)
    for w0 in range(0,NW,4):
        ws=range(w0,w0+4)
        sd={}
        for w in ws:
            sl=pl.ds(w*WT,WT)
            q=qkvc_ref[sl,0:128]; k=qkvc_ref[sl,128:256]; v=qkvc_ref[sl,256:384]; c=qkvc_ref[sl,384:512]
            sd[w]=(dnt(two(k),q),dnt(two(v),c))
        pd={}
        for w in ws:
            s2,d2=sd[w]
            ps=[];dss=[]
            for h in range(2):
                s=s2[WT*h:WT*h+WT]
                mx=jnp.max(s,axis=0,keepdims=True)
                e=jnp.exp2((s-mx)*(0.125*LOG2E))
                wt=e*(1.0/jnp.sum(e,axis=0,keepdims=True))
                p=wt.astype(bf16)
                dp=d2[WT*h:WT*h+WT].astype(bf16).astype(f32)
                t=wt*dp
                ds=(t-wt*jnp.sum(t,axis=0,keepdims=True)).astype(bf16)
                ps.append(p);dss.append(ds)
            pd[w]=(ps,dss)
        for w in ws:
            sl=pl.ds(w*WT,WT)
            ps,dss=pd[w]
            q=qkvc_ref[sl,0:128]; k=qkvc_ref[sl,128:256]; v=qkvc_ref[sl,256:384]; c=qkvc_ref[sl,384:512]
            kt=k.T; vt=v.T
            cts=[dot(vt[:64],ps[0]),dot(vt[64:],ps[1])]
            dqs=[dot(kt[:64],dss[0]),dot(kt[64:],dss[1])]
            dv=jnp.where(lo,dot(ps[0],c),dot(ps[1],c))
            dk=jnp.where(lo,dot(dss[0],q),dot(dss[1],q))
            ctx=jnp.concatenate(cts,0).astype(bf16)
            go=go+dot(ctx,back_ref[sl,:])
            dq=(jnp.concatenate(dqs,0)*0.125).astype(bf16).T
            d_ref[sl,0:128]=dq
            d_ref[sl,128:256]=(dk*0.125).astype(bf16)
            d_ref[sl,256:384]=dv.astype(bf16)
    go_store((go*scale).astype(bf16))
    g_store((dot(nt_ref[...],d_ref[...])*scale).astype(bf16))
    dn=dnt(d_ref[...],W)
    dn_ref[...]=jnp.where(first,0.0,dn_ref[...])+dn
def tail_norm(dn_ref,xh_ref,rstd_ref,gain_ref,back_ref,dwin_ref):
    gain=gain_ref[...]
    for w in range(NW):
        sl=pl.ds(w*WT,WT)
        dx=dn_ref[sl,:].astype(bf16).astype(f32)*gain
        xh=xh_ref[sl,:]
        d=rstd_ref[sl,:]*(dx-jnp.mean(dx,-1,keepdims=True)-xh*jnp.mean(dx*xh,-1,keepdims=True))
        dwin_ref[sl,:]=(back_ref[sl,:].astype(f32)+d).astype(bf16)

def tail_put(order_ref,dwin_ref,out_ref):
    row=order_ref[...]
    T=row.shape[1]
    for w in range(NW):
        sl=pl.ds(w*WT,WT)
        si=lax.broadcasted_iota(jnp.int32,(WT,T),0)+w*WT
        oh=jnp.where(si==row,1.0,0.0).astype(bf16)
        out_ref[sl,:]=dot(oh,dwin_ref[...]).astype(bf16)


def remote(src, dst, ss, rs, dev):
    return pltpu.make_async_remote_copy(
        src_ref=src, dst_ref=dst, send_sem=ss, recv_sem=rs, device_id=dev, device_id_type=MESH
    )


def split3(v):
    a = v.astype(bf16)
    r = v - a.astype(f32)
    b = r.astype(bf16)
    c = (r - b.astype(f32)).astype(bf16)
    return jnp.concatenate([a, b, c], 0)


def pieces(v):
    a = v.astype(bf16)
    r = v - a.astype(f32)
    b = r.astype(bf16)
    return a, b, (r - b.astype(f32)).astype(bf16)


def hdot(a, b):
    rows = a.shape[0]
    b1, b2, b3 = pieces(b)
    a3 = split3(a)
    u = dot(a3, b1)
    v = dot(a3[: 2 * rows], b2)
    w = dot(a3[:rows], b3)
    return u[:rows] + ((u[rows : 2 * rows] + v[:rows]) + (u[2 * rows :] + (v[rows:] + w)))


def inverse_factors(gram):
    lane = lax.broadcasted_iota(jnp.int32, (32, 128), 1)
    row = lax.broadcasted_iota(jnp.int32, (32, 128), 0)
    first = (lane % 64) < 32
    state = jnp.where(lane < 64, gram, jnp.where((lane % 32) == row, 1.0, 0.0))
    for j in range(31):
        cols = jnp.where(first, state[:, j : j + 1], state[:, 32 + j : 33 + j])
        factor = cols / cols[j : j + 1, :]
        state = state - jnp.where(row > j, factor, 0.0) * state[j : j + 1, :]
    out = []
    for k in range(2):
        diag = jnp.sum(jnp.where(lane == row + 32 * k, state, 0.0), axis=1, keepdims=True)
        out.append(state[:, 64 + 32 * k : 96 + 32 * k] * (1.0 / jnp.sqrt(diag)))
    return out


def kernel(
    scale,
    order_in, tok_in, cot_in, gain_in, w_in, wo_in, errq_in, erro_in, qq_in, qo_in,
    dtok_ref, R, left_ref, inv_ref, mq, mo,
    order_ref, tok_ref, cot_ref, gain_ref, w_ref, wo_ref, errq_ref, erro_ref, qq_ref, qo_ref, in_sem,
    W, WO, back, n, nt, xh, rstd, d, dn, qkvc,
    gbuf, xr, xm, zs, zr, gobuf, xro, xmo, zso, zro,
    lr, mb, mr, t1, ex, ez, S, bqi, boi,
    az_s, az_r, ax_s, ax_r, ay_s, ay_r, ac_s, ac_r,
    rx_s, rx_r, rz_s, rz_r, ro_s,
    l_s, l_r, e_s, e_r,
):
    r = lax.axis_index("rep")
    f = lax.axis_index("fsdp")
    y = r // 2
    c = r % 2
    z = f // 4
    x = f % 4

    def zp(dz):
        return (r, ((z + dz) % 8) * 4 + x)

    def xp(dx):
        return (r, z * 4 + (x + dx) % 4)

    def yp(dy):
        return (((y + dy) % 4) * 2 + c, f)

    cp = (y * 2 + 1 - c, f)

    def rp(k):
        return ((r + k) % 8, f)

    loads = [
        pltpu.make_async_copy(a, b, in_sem.at[k])
        for k, (a, b) in enumerate(
            (
                (w_in, w_ref), (wo_in, wo_ref), (order_in, order_ref), (gain_in, gain_ref), (tok_in, tok_ref),
                (cot_in, cot_ref), (errq_in, errq_ref), (erro_in, erro_ref), (qq_in, qq_ref), (qo_in, qo_ref),
            )
        )
    ]
    for cc in loads:
        cc.start()
    barrier = pltpu.get_barrier_semaphore()
    for k in range(1, 8):
        pl.semaphore_signal(barrier, inc=1, device_id=zp(k), device_id_type=MESH)
        pl.semaphore_signal(barrier, inc=1, device_id=rp(k), device_id_type=MESH)
    for k in range(1, 4):
        pl.semaphore_signal(barrier, inc=1, device_id=xp(k), device_id_type=MESH)

    def fr(w):
        front_window(w, order_ref, tok_ref, cot_ref, gain_ref, back, n, xh, rstd)

    source = (x // 2) == c
    for cc in loads[:2]:
        cc.wait()

    own = y % 2

    @pl.when(source)
    def _():
        for i in range(2):
            for k in range(3):
                W[2 * own + i, z, x, :, 128 * k : 128 * k + 128] = w_ref[
                    :, pl.ds(pl.multiple_of(512 * k + (2 * own + i) * 128, 128), 128)
                ]

        @pl.when((z // 4) == own)
        def _():
            WO[z, x] = wo_ref[...]

    pl.semaphore_wait(barrier, 17)

    def w_z(i, k, at):
        a = W.at[2 * own + i, at, x]
        return remote(a, a, az_s.at[i, k - 1], az_r.at[i, k - 1], zp(k))

    def wo_z(k, at):
        a = WO.at[at, x]
        return remote(a, a, az_s.at[2, k - 1], az_r.at[2, k - 1], zp(k))

    def w_x(i, k, at):
        a = W.at[2 * own + i, :, at]
        b = WO.at[pl.ds(2 * (2 * own + i), 2), at]
        return (
            remote(a, a, ax_s.at[0, i, k - 1], ax_r.at[0, i, k - 1], xp(k)),
            remote(b, b, ax_s.at[1, i, k - 1], ax_r.at[1, i, k - 1], xp(k)),
        )

    def wait_x(i):
        for k in range(1, 4):
            src = (x - k + 4) % 4

            @pl.when((src // 2) == c)
            def _():
                for cc in w_x(i, k, src):
                    cc.wait_recv()

    @pl.when(source)
    def _():
        for i in range(2):
            for k in FAR:
                w_z(i, k, z).start()
            if i == 0:

                @pl.when((z // 4) == own)
                def _():
                    for k in range(1, 8):
                        wo_z(k, z).start()

    for cc in loads[2:6]:
        cc.wait()
    fr(0)
    fr(1)
    fr(2)

    @pl.when(source)
    def _():
        for i in range(2):
            for k in range(1, 8):
                src = (z - k + 8) % 8
                w_z(i, k, src).wait_recv()

                @pl.when((src // 2) == 2 * own + i)
                def _():
                    wo_z(k, src).wait_recv()

            for k in range(1, 4):
                for cc in w_x(i, k, x):
                    cc.start()

    fr(3)
    nt[...] = n[...].T

    def hp_of(s):
        return (2 * own + s) % 4

    def half(hp, core):
        return W.at[hp, :, pl.ds(2 * core, 2)], WO.at[pl.ds(2 * hp, 2), pl.ds(2 * core, 2)]

    def core_copy(s, core):
        a, b = half(hp_of(s), core)
        return (
            remote(a, a, ac_s.at[0, s], ac_r.at[0, s], cp),
            remote(b, b, ac_s.at[1, s], ac_r.at[1, s], cp),
        )

    def y_copy(i, hp):
        out = []
        for way in range(2):
            a = W.at[hp, pl.ds(4 * way, 4), pl.ds(2 * c, 2)]
            b = WO.at[pl.ds(2 * hp + way, 1), pl.ds(2 * c, 2)]
            to = yp(1 + 2 * way)
            out.append(remote(a, a, ay_s.at[0, i, way], ay_r.at[0, i, way], to))
            out.append(remote(b, b, ay_s.at[1, i, way], ay_r.at[1, i, way], to))
        return out

    def spread(i):
        wait_x(i)
        for cc in y_copy(i, 2 * own + i):
            cc.start()
        for cc in core_copy(i, c):
            cc.start()

    spread(0)

    def x_copy(kind, s, way):
        to = xp(1 + 2 * way)
        h = 1 - way if kind == 1 else way
        if kind == 2:
            a, b = xm.at[s, way], xmo.at[s, pl.ds(way, 1)]
        else:
            at = (x + 2) % 4 if kind == 0 else (x + 1 + 2 * way) % 4
            a, b = gbuf.at[s, pl.ds(4 * h, 4), at], gobuf.at[s, pl.ds(h, 1), at]
        return (
            remote(a, xr.at[kind, s, way], rx_s.at[0, kind, s, way], rx_r.at[0, kind, s, way], to),
            remote(b, xro.at[kind, s, pl.ds(way, 1)], rx_s.at[1, kind, s, way], rx_r.at[1, kind, s, way], to),
        )

    def merge(s):
        for way in range(2):
            for cc in x_copy(0, s, way):
                cc.wait_recv()
            at = (x + 1 + 2 * way) % 4
            xm[s, way] = (gbuf[s, 4 * way : 4 * way + 4, at].astype(f32) + xr[0, s, way].astype(f32)).astype(bf16)
            xmo[s, way] = (gobuf[s, way, at].astype(f32) + xro[0, s, way].astype(f32)).astype(bf16)
            for cc in x_copy(2, s, way):
                cc.start()

    def z_send(s, k):
        return remote(
            zs.at[s, (z + k) % 8], zr.at[s, k - 1], rz_s.at[0, s, k - 1], rz_r.at[0, s, k - 1], zp(k)
        )

    def zo_send(s, j, k):
        return remote(zso.at[s, j], zro.at[k - 1], ro_s.at[s, j], rz_r.at[1, 0, k - 1], zp(k))

    def zo_each(s, act):
        for j in range(2):
            k = (2 * hp_of(s) + j - z + 8) % 8

            @pl.when(k > 0)
            def _():
                act(zo_send(s, j, k))

    def second(s):
        for kind in (1, 2):
            for way in range(2):
                for cc in x_copy(kind, s, way):
                    cc.wait_recv()
        for h in range(2):
            rows = slice(4 * h, 4 * h + 4)
            total = gbuf[s, rows, x].astype(f32) + (xr[1, s, 1 - h].astype(f32) + xr[2, s, h].astype(f32))
            zs[s, rows] = total.astype(bf16)
            total = gobuf[s, h, x].astype(f32) + (xro[1, s, 1 - h].astype(f32) + xro[2, s, h].astype(f32))
            zso[s, h] = total.astype(bf16)
        for k in FAR:
            z_send(s, k).start()
        zo_each(s, lambda cc: cc.start())

    def step(s, carry):
        hp = hp_of(s)
        for cc in core_copy(s, 1 - c):
            cc.wait_recv()

        def mid():
            @pl.when(s == 0)
            def _():
                spread(1)

            @pl.when((s == 1) | (s == 2))
            def _():
                for cc in y_copy(s - 1, hp_of(s + 1)):
                    cc.wait_recv()
                for cc in core_copy(s + 1, c):
                    cc.start()

        def g_store(v):
            gbuf[s] = v.reshape(8, 4, 16, 384)

        def go_store(v):
            gobuf[s] = v.reshape(2, 4, 16, 512)

        pair(
            n, nt, back, W[hp].reshape(512, 384), WO[pl.ds(2 * hp, 2)].reshape(128, 512),
            d, dn, qkvc, scale, s == 0, g_store, go_store, mid,
        )
        for kind in (0, 1):
            for way in range(2):
                for cc in x_copy(kind, s, way):
                    cc.start()

        @pl.when(s > 0)
        def _():
            merge(s - 1)

        @pl.when(s > 1)
        def _():
            second(s - 2)

        return carry

    lax.fori_loop(0, 4, step, 0)

    merge(3)
    second(2)
    second(3)
    tail_norm(dn, xh, rstd, gain_ref, back, qkvc)
    tail_put(order_ref, qkvc, dtok_ref)

    for cc in loads[6:]:
        cc.wait()
    q = qq_ref[...].astype(f32).astype(bf16)
    zero = jnp.zeros((32, 1536), bf16)
    bqi[...] = jnp.concatenate([q, zero, q, zero], 0)
    q = qo_ref[...].astype(f32).astype(bf16)
    zero = jnp.zeros((32, 512), bf16)
    boi[...] = jnp.concatenate([zero, q, zero, q], 0)

    def collect(s, carry):
        hp = hp_of(s)
        total = zs[s, z].astype(f32)
        for k in range(1, 8):
            z_send(s, k).wait_recv()
            total = total + zr[s, k - 1].astype(f32)
        for k in range(3):
            at = pl.ds(pl.multiple_of(512 * k + hp * 128, 128), 128)
            mq[:, at] = total[:, 128 * k : 128 * k + 128] + errq_ref[:, at]
        return carry

    lax.fori_loop(0, 4, collect, 0)
    for k in range(1, 8):
        zo_send(0, 0, k).wait_recv()
    so = (z // 2 - 2 * own + 4) % 4
    total = zso[so, z % 2].astype(f32)
    for k in range(7):
        total = total + zro[k].astype(f32)
    mo[...] = total + erro_ref[...]

    mqv = mq[...]
    mov = mo[...]
    def m_copy(k):
        return remote(mb.at[(r + k) % 8], mr.at[k - 1], l_s.at[1, k - 1], l_r.at[1, k - 1], rp(k))

    def l_copy(k, at):
        return remote(lr.at[at], lr.at[at], l_s.at[0, k - 1], l_r.at[0, k - 1], rp(k))

    part = dnt(split3(mqv), bqi[...]) + dnt(split3(mov), boi[...])
    part = ((part[0:16] + part[16:32]) + part[32:48]) * (1.0 / 127.0)
    low = lax.broadcasted_iota(jnp.int32, (8, 128), 1) < 64
    lr[r] = jnp.where(low, part[0:8], part[8:16])
    for k in FAR:
        l_copy(k, r).start()
    for k in range(12):
        mb[k // 2, k % 2] = mqv[:, 128 * k : 128 * k + 128]
    for k in range(4):
        mb[6 + k // 2, k % 2] = mov[:, 128 * k : 128 * k + 128]
    for k in FAR:
        m_copy(k).start()
    for k in range(1, 8):
        m_copy(k).wait_recv()
    total = mb[r]
    for k in range(7):
        total = total + mr[k]
    for k in range(1, 8):
        l_copy(k, (r - k + 8) % 8).wait_recv()
    left = lr[0]
    for k in range(1, 8):
        left = left + lr[k]
    left = left * 0.125
    turned = pltpu.roll(left, 64, 1)
    left = jnp.concatenate([jnp.where(low, left, turned), jnp.where(low, turned, left)], 0)
    left_ref[...] = left

    lt = left.T
    lane = lax.broadcasted_iota(jnp.int32, (16, 128), 1)
    full = hdot(lt, left)
    gram = jnp.where(
        lane < 64,
        jnp.where(lane < 32, full[0:16], full[32:48]),
        jnp.where(lane < 96, full[16:32], full[48:64]),
    )
    mine = jnp.where(r < 6, lt[0:32], lt[32:64])
    for j in range(2):
        t = hdot(mine, total[j])
        for k in range(2):
            t1[2 * j + k, 0:16] = t[16 * k : 16 * k + 16]
            t1[2 * j + k, 16:24] = gram[8 * k : 8 * k + 8]
    ex[x] = t1[x]

    def e_x(k, to, at):
        return remote(t1.at[to], ex.at[at], e_s.at[0, k - 1], e_r.at[0, k - 1], xp(k))

    def e_z(k, at):
        return remote(ez.at[at], ez.at[at], e_s.at[1, k - 1], e_r.at[1, k - 1], zp(k))

    def a_x(k, at):
        return remote(S.at[at], S.at[at], e_s.at[2, k - 1], e_r.at[2, k - 1], xp(k))

    def a_r(k, at):
        return remote(R.at[at], R.at[at], e_s.at[3, k - 1], e_r.at[3, k - 1], rp(k))

    for k in (2, 1, 3):
        e_x(k, (x + k) % 4, x).start()
    for k in range(1, 4):
        e_x(k, x, (x - k + 4) % 4).wait_recv()
    ez[z] = (ex[0] + ex[1]) + (ex[2] + ex[3])
    for k in FAR:
        e_z(k, z).start()
    for k in range(1, 8):
        e_z(k, (z - k + 8) % 8).wait_recv()
    total = ez[0]
    for k in range(1, 8):
        total = total + ez[k]
    S[x] = total
    for k in (2, 1, 3):
        a_x(k, x).start()
    for k in range(1, 4):
        a_x(k, (x - k + 4) % 4).wait_recv()
    R[r] = S[:, 0:16]
    for k in FAR:
        a_r(k, r).start()
    gram = jnp.concatenate([S[0, 16:24], S[1, 16:24]], 0)
    iq, io = inverse_factors(jnp.concatenate([gram, pltpu.roll(gram, 64, 1)], 0))
    inv_ref[0] = iq
    inv_ref[1] = io
    for k in range(1, 8):
        a_r(k, (r - k + 8) % 8).wait_recv()

    @pl.when(source)
    def _():
        for i in range(2):
            for k in range(1, 8):
                w_z(i, k, z).wait_send()
            for k in range(1, 4):
                for cc in w_x(i, k, x):
                    cc.wait_send()

        @pl.when((z // 4) == own)
        def _():
            for k in range(1, 8):
                wo_z(k, z).wait_send()

    for i in range(2):
        for cc in y_copy(i, 2 * own + i):
            cc.wait_send()

    def sent(s, carry):
        for cc in core_copy(s, c):
            cc.wait_send()
        for kind in range(3):
            for way in range(2):
                for cc in x_copy(kind, s, way):
                    cc.wait_send()
        for k in range(1, 8):
            z_send(s, k).wait_send()
        zo_each(s, lambda cc: cc.wait_send())
        return carry

    lax.fori_loop(0, 4, sent, 0)
    for k in range(1, 8):
        m_copy(k).wait_send()
        l_copy(k, r).wait_send()
        e_z(k, z).wait_send()
        a_r(k, r).wait_send()
    for k in range(1, 4):
        e_x(k, (x + k) % 4, x).wait_send()
        a_x(k, x).wait_send()


def finish(
    dtok_in, R, left_ref, inv_ref, mq_ref, mo_ref,
    dtok_out, gradq_out, grado_out, nerrq_out, nerro_out, bq_out, bo_out,
    gradq, grado, nerrq, nerro, bq, bo, sem,
):
    def out(k, a, b):
        cc = pltpu.make_async_copy(a, b, sem.at[k])
        cc.start()
        return cc

    outs = [out(0, dtok_in, dtok_out)]
    left = left_ref[...]
    iq = inv_ref[0]
    io = inv_ref[1]
    ortho_q = hdot(left[:, 0:32], iq.T)
    ortho_o = hdot(left[:, 32:64], io.T)
    blocks = R[...].reshape(16, 32, 128)
    bq[...] = hdot(iq, jnp.concatenate([blocks[k] for k in range(12)], 1)) * 0.125
    outs.append(out(1, bq, bq_out))
    bo[...] = hdot(io, jnp.concatenate([blocks[12 + k] for k in range(4)], 1)) * 0.125
    outs.append(out(2, bo, bo_out))
    grad = hdot(ortho_q, bq[...])
    gradq[...] = grad
    nerrq[...] = mq_ref[...] - grad
    outs.append(out(3, gradq, gradq_out))
    outs.append(out(4, nerrq, nerrq_out))
    grad = hdot(ortho_o, bo[...])
    grado[...] = grad
    nerro[...] = mo_ref[...] - grad
    outs.append(out(5, grado, grado_out))
    outs.append(out(6, nerro, nerro_out))
    for cc in outs:
        cc.wait()


def per_device(tokens, cotangent, window_order, gain, w_qkv, w_out, err_qkv, err_out, q_qkv, q_out):
    scale = float(lax.axis_size("fsdp") * tokens.shape[0]) ** (-0.5)
    vmem = pl.BlockSpec(memory_space=pltpu.VMEM)
    V = pltpu.VMEM
    dma = pltpu.SemaphoreType.DMA
    hbm = pl.BlockSpec(memory_space=pl.ANY)

    def shape(dims, kind=f32):
        return jax.ShapeDtypeStruct(dims, kind)

    mid = pl.pallas_call(
        functools.partial(kernel, scale),
        out_shape=(
            shape((576, 512), bf16), shape((8, 4, 16, 128)), shape((16, 128)), shape((2, 32, 32)),
            shape((16, 1536)), shape((16, 512)),
        ),
        in_specs=[hbm] * 10,
        out_specs=(vmem,) * 6,
        scratch_shapes=[
            V((1, 576), jnp.int32), V((576, 512), bf16), V((576, 512), bf16), V((1, 512), f32),
            V((16, 1536), bf16), V((16, 512), bf16), V((16, 1536), f32), V((16, 512), f32),
            V((32, 1536), jnp.int32), V((32, 512), jnp.int32), dma((10,)),
            V((4, 8, 4, 16, 384), bf16), V((8, 4, 16, 512), bf16),
            V((576, 512), bf16), V((576, 512), bf16), V((512, 576), bf16),
            V((576, 512), f32), V((576, 1), f32), V((576, 384), bf16), V((576, 512), f32), V((576, 512), bf16),
            V((4, 8, 4, 16, 384), bf16), V((3, 4, 2, 4, 16, 384), bf16), V((4, 2, 4, 16, 384), bf16), V((4, 8, 16, 384), bf16), V((4, 7, 16, 384), bf16),
            V((4, 2, 4, 16, 512), bf16), V((3, 4, 2, 16, 512), bf16), V((4, 2, 16, 512), bf16), V((4, 2, 16, 512), bf16), V((7, 16, 512), bf16),
            V((8, 8, 128), f32), V((8, 2, 16, 128), f32), V((7, 2, 16, 128), f32),
            V((4, 24, 128), f32), V((4, 24, 128), f32), V((8, 24, 128), f32), V((4, 24, 128), f32),
            V((128, 1536), bf16), V((128, 512), bf16),
            dma((3, 7)), dma((3, 7)), dma((2, 2, 3)), dma((2, 2, 3)), dma((2, 2, 2)), dma((2, 2, 2)), dma((2, 4)), dma((2, 4)),
            dma((2, 3, 4, 2)), dma((2, 3, 4, 2)), dma((1, 4, 7)), dma((2, 4, 7)), dma((4, 2)),
            dma((2, 7)), dma((2, 7)), dma((4, 7)), dma((4, 7)),
        ],
        compiler_params=pltpu.CompilerParams(
            collective_id=0, has_side_effects=True, vmem_limit_bytes=56 * 2**20
        ),
    )(
        window_order, tokens, cotangent, gain.reshape(1, 512), w_qkv, w_out,
        err_qkv.reshape(16, 1536), err_out.reshape(16, 512), q_qkv.T, q_out.T,
    )
    dt, gq, go, eq, eo, bq, bo = pl.pallas_call(
        finish,
        out_shape=(
            shape((576, 512), bf16), shape((16, 1536)), shape((16, 512)), shape((16, 1536)), shape((16, 512)),
            shape((32, 1536)), shape((32, 512)),
        ),
        in_specs=[vmem] * 6,
        out_specs=(hbm,) * 7,
        scratch_shapes=[
            V((16, 1536), f32), V((16, 512), f32), V((16, 1536), f32), V((16, 512), f32),
            V((32, 1536), f32), V((32, 512), f32), dma((7,)),
        ],
    )(*mid)
    return dt, gq, go, eq[None], eo[None], bq.T, bo.T


def solution(mesh):
    return jax.shard_map(
        per_device,
        mesh=mesh,
        in_specs=(
            P(("rep", "fsdp"), None),
            P(("rep", "fsdp"), None),
            P(("rep", "fsdp"), None),
            P(),
            P("fsdp", None),
            P("fsdp", None),
            P("rep", "fsdp", None),
            P("rep", "fsdp", None),
            P(),
            P(),
        ),
        out_specs=(
            P(("rep", "fsdp"), None),
            P("fsdp", None),
            P("fsdp", None),
            P("rep", "fsdp", None),
            P("rep", "fsdp", None),
            P(),
            P(),
        ),
        check_vma=False,
    )
```
